32 devices in a mesh: lon: 8 (over z, x), lat: 4 (over y, core).
Axes of the slice: x: 2, y: 2, z: 4, core: 2. Of those that a mesh axis runs over, the one named last changes fastest.
Arguments:
- ensemble: bfloat16 [40, 2, 512, 2048], P(None, None, 'lat', 'lon'), may hold values from -6 to 6
- gradient: bfloat16 [2, 512, 2048], P(None, 'lat', 'lon'), may hold values from -6 to 6
Outputs:
- control: bfloat16 [40, 2, 512, 2048], P(None, None, 'lat', 'lon')
The draws below stay inside these ranges and needn't reach their ends.
All inputs are finite; a program needn't handle non-finite values.
Results may differ from the reference program's by a relative error of at most 0.0073.
Values may be sent and summed in bfloat16 or wider, within the bound.
No kernel may reach another device: no remote copies, remote signals or barrier semaphores. Data moves between devices by JAX's collectives and lax.ppermute only.
A program may use at most 128 MiB of HBM per device.

```python
import jax
import jax.numpy as jnp
from jax import lax

MEMBERS = 40
LEV = 2
HALF = 30
LON_DEV = 256
LAT_DEV = 128
NLON = 2048
NLAT = 512


def level_of(stream_key, extent, cuts, least, high):
    def one(position, parts):
        steps = jax.random.uniform(jax.random.fold_in(jax.random.fold_in(stream_key, 6), position), (parts,), jnp.float32, least / len(cuts), high / len(cuts))
        return jnp.repeat(jnp.exp(steps), extent[position] // parts).reshape((-1,) + (1,) * (len(extent) - position - 1))

    level = one(*cuts[0])
    for cut in cuts[1:]:
        level = level * one(*cut)
    return level


def noise(rng, dims, scale, most, pieces=(), kind=jnp.bfloat16):
    result = jax.random.normal(rng, dims, jnp.float32) * scale
    if len(pieces) > 0:
        result = level_of(rng, dims, pieces, -0.22, 0.18) * result
    return jnp.clip(result, min=-most, max=most).astype(kind)


def setup_inputs(seed: int = 0) -> dict:
    splits = jax.random.split(jax.random.key(seed), 3)
    return {
        "ensemble": noise(splits[0], (MEMBERS, LEV, NLAT, NLON), 1.0, 6.0, ((2, 4), (3, 8))),
        "gradient": noise(splits[1], (LEV, NLAT, NLON), 1.0, 6.0, ((1, 4), (2, 8))),
    }


def kernel_matrix(block_len, half_width):
    spread = 1.0 * half_width
    row_index = jnp.arange(block_len + 2 * half_width)[:, None]
    col_index = jnp.arange(block_len)[None, :]
    offset = (row_index - col_index - half_width).astype(jnp.float32)
    offsets = jnp.arange(-half_width, half_width + 1).astype(jnp.float32)
    normalizer = jnp.sqrt(jnp.sum(jnp.exp(-offsets * offsets / (spread * spread))))
    weights = jnp.where(jnp.abs(offset) <= half_width, jnp.exp(-offset * offset / (2.0 * spread * spread)), 0.0) / normalizer
    return weights.astype(jnp.bfloat16)

def reference(ensemble, gradient):
    lon_kernel = kernel_matrix(LON_DEV, HALF).astype(jnp.float32)
    lat_kernel = kernel_matrix(LAT_DEV, HALF).astype(jnp.float32)
    gradient_f32 = gradient.astype(jnp.float32)
    highest = lax.Precision.HIGHEST

    def member(perturbation):
        product = (perturbation.astype(jnp.float32) * gradient_f32).astype(jnp.bfloat16)
        product = lax.optimization_barrier(product).astype(jnp.float32)
        lon_blocks = NLON // LON_DEV
        filler = jnp.zeros((LEV, NLAT, LON_DEV - 2 * HALF), jnp.float32)
        padded = jnp.concatenate([product[:, :, NLON - HALF:], product, product[:, :, :HALF], filler], axis=2)
        blocks = padded.reshape(LEV, NLAT, lon_blocks + 1, LON_DEV)
        lon_done = jnp.einsum('lanp,pq->lanq', blocks[:, :, :-1], lon_kernel[:LON_DEV], precision=highest)
        lon_done = lon_done + jnp.einsum('lanp,pq->lanq', blocks[:, :, 1:, :2 * HALF], lon_kernel[LON_DEV:], precision=highest)
        lon_done = lon_done.reshape(LEV, NLAT, NLON).astype(jnp.bfloat16)
        lon_done = lax.optimization_barrier(lon_done).astype(jnp.float32)
        lat_blocks = NLAT // LAT_DEV
        padded = jnp.pad(lon_done, ((0, 0), (HALF, LAT_DEV - HALF), (0, 0)))
        blocks = padded.reshape(LEV, lat_blocks + 1, LAT_DEV, NLON)
        across = jnp.einsum('lnpc,pq->lnqc', blocks[:, :-1], lat_kernel[:LAT_DEV], precision=highest)
        across = across + jnp.einsum('lnpc,pq->lnqc', blocks[:, 1:, :2 * HALF], lat_kernel[LAT_DEV:], precision=highest)
        return across.reshape(LEV, NLAT, NLON).astype(jnp.bfloat16)
    return lax.map(member, ensemble)
```

```python
import jax
import jax.numpy as jnp
import numpy as np
from jax import lax
from jax.experimental import pallas as pl
from jax.experimental.pallas import tpu as pltpu
from jax.sharding import PartitionSpec as P

HALF = 30
LANES = 128
EDGE = 32
GROUP = 17
VMEM = 48 * 1024 * 1024


def taps():
    offsets = np.arange(-HALF, HALF + 1).astype(np.float32)
    spread = np.float32(HALF)
    norm = np.sqrt(np.sum(np.exp(-offsets * offsets / (spread * spread)), dtype=np.float32))
    return (np.exp(-offsets * offsets / (2 * spread * spread)) / norm).astype(jnp.bfloat16)


def band(block_len, margin):
    k = taps()
    out = np.zeros((block_len + 2 * margin, block_len), jnp.bfloat16)
    for q in range(block_len):
        out[q + margin - HALF : q + margin + HALF + 1, q] = k
    return out


def lane_of(slot, j):
    if slot < 4:
        return HALF * slot + j
    lane = j - 8 * (slot - 4)
    return 120 + lane if 0 <= lane < 8 else None


def lon_constants(width):
    lon = band(width, HALF)
    select = np.zeros((8, width, 2 * LANES), jnp.bfloat16)
    spread = np.zeros((8, 2 * LANES, width), jnp.bfloat16)
    for s in range(8):
        for j in range(HALF):
            lane = lane_of(s, j)
            if lane is None:
                continue
            select[s, width - HALF + j, lane] = 1
            select[s, j, LANES + lane] = 1
            spread[s, lane] = lon[j]
            spread[s, LANES + lane] = lon[width + HALF + j]
    return select, spread, lon[HALF : HALF + width]


def dot(a, b):
    return jnp.dot(a, b, preferred_element_type=jnp.float32)


def product(ens, grad):
    return (ens.astype(jnp.float32) * grad.astype(jnp.float32)).astype(jnp.bfloat16)


def products(ens_ref, grad_ref, first, count):
    grads = [grad_ref[0], grad_ref[1]]
    even = lax.rem(first, 2) == 0
    flip = [jnp.where(even, grads[0], grads[1]), jnp.where(even, grads[1], grads[0])]
    return [product(ens_ref[i], flip[i % 2]) for i in range(count)]


def pack_group(fields, select_ref, right_ref, left_ref):
    rows = fields[0].shape[0]
    extra = dot(fields[16], select_ref[4])
    extras = [extra] + [dot(fields[16], select_ref[4 + t]) for t in range(1, 4)]
    acc = jnp.concatenate(extras, axis=0)
    for s in range(4):
        acc += dot(jnp.concatenate(fields[4 * s : 4 * s + 4], axis=0), select_ref[s])
    acc = acc.astype(jnp.bfloat16)
    for t in range(4):
        tile = acc[t * rows : (t + 1) * rows]
        right_ref[t] = tile[:, :LANES]
        left_ref[t] = tile[:, LANES:]


def spread_group(fields, low_ref, high_ref, center, spread_ref):
    rows = fields[0].shape[0]
    tiles = [jnp.concatenate([low_ref[t], high_ref[t]], axis=1) for t in range(4)]
    halo = jnp.concatenate(tiles, axis=0)
    out = []
    for s in range(4):
        block = dot(jnp.concatenate(fields[4 * s : 4 * s + 4], axis=0), center)
        block = (block + dot(halo, spread_ref[s])).astype(jnp.bfloat16)
        out += [block[t * rows : (t + 1) * rows] for t in range(4)]
    last = dot(fields[16], center)
    for t in range(4):
        last += dot(tiles[t], spread_ref[4 + t])
    return out + [last.astype(jnp.bfloat16)]


def pack_kernel(ens_ref, grad_ref, select_ref, right_ref, left_ref):
    fields = products(ens_ref, grad_ref, pl.program_id(0) * GROUP, GROUP)
    pack_group(fields, select_ref, right_ref, left_ref)


def rows_kernel(first, head_ref, tail_ref, ghead_ref, gtail_ref, up_ref, down_ref):
    start = first + pl.program_id(0) * head_ref.shape[0]
    for i, v in enumerate(products(head_ref, ghead_ref, start, head_ref.shape[0])):
        down_ref[i] = v
    for i, v in enumerate(products(tail_ref, gtail_ref, start, head_ref.shape[0])):
        up_ref[i] = v


def lat_group(fields, low_ref, high_ref, lat):
    out = []
    for i, v in enumerate(fields):
        wide = jnp.concatenate([low_ref[i], v, high_ref[i]], axis=0)
        out.append(dot(lat, wide).astype(jnp.bfloat16))
    return out


def lat_pack_kernel(first, ens_ref, grad_ref, low_ref, high_ref, lat_ref, select_ref, done_ref, right_ref, left_ref):
    start = first + pl.program_id(0) * GROUP
    fields = products(ens_ref, grad_ref, start, GROUP)
    fields = lat_group(fields, low_ref, high_ref, lat_ref[...])
    for i, v in enumerate(fields):
        done_ref[i] = v
    pack_group(fields, select_ref, right_ref, left_ref)


def lat_pack4_kernel(first, ens_ref, grad_ref, low_ref, high_ref, lat_ref, select_ref, done_ref, right_ref, left_ref):
    fields = products(ens_ref, grad_ref, jnp.int32(first), 4)
    fields = lat_group(fields, low_ref, high_ref, lat_ref[...])
    acc = None
    for s, v in enumerate(fields):
        done_ref[s] = v
        part = dot(v, select_ref[s])
        acc = part if acc is None else acc + part
    acc = acc.astype(jnp.bfloat16)
    right_ref[0] = acc[:, :LANES]
    left_ref[0] = acc[:, LANES:]


def lon_kernel(ens_ref, grad_ref, low_ref, high_ref, center_ref, spread_ref, done_ref, up_ref, down_ref):
    fields = products(ens_ref, grad_ref, pl.program_id(0) * GROUP, GROUP)
    for i, v in enumerate(spread_group(fields, low_ref, high_ref, center_ref[...], spread_ref)):
        done_ref[i] = v
        down_ref[i] = v[:EDGE]
        up_ref[i] = v[v.shape[0] - EDGE :]


def lat_kernel(done_ref, low_ref, high_ref, lat_ref, out_ref):
    fields = [done_ref[i] for i in range(GROUP)]
    for i, v in enumerate(lat_group(fields, low_ref, high_ref, lat_ref[...])):
        out_ref[i] = v


def last_kernel(done_ref, low_ref, high_ref, center_ref, spread_ref, whole_ref, out_ref):
    del whole_ref
    fields = [done_ref[i] for i in range(GROUP)]
    for i, v in enumerate(spread_group(fields, low_ref, high_ref, center_ref[...], spread_ref)):
        out_ref[i] = v


def last4_kernel(done_ref, low_ref, high_ref, center_ref, spread_ref, whole_ref, out_ref):
    del whole_ref
    halo = jnp.concatenate([low_ref[0], high_ref[0]], axis=1)
    for s in range(4):
        out_ref[s] = (dot(done_ref[s], center_ref[...]) + dot(halo, spread_ref[s])).astype(jnp.bfloat16)


def neighbours(axis, periodic):
    count = lax.axis_size(axis)
    forward = [(i, i + 1) for i in range(count - 1)]
    if periodic:
        forward.append((count - 1, 0))
    return forward, [(b, a) for a, b in forward]


def exchange(up, down, axis, periodic):
    forward, backward = neighbours(axis, periodic)
    return lax.ppermute(up, axis, forward), lax.ppermute(down, axis, backward)


def whole(*shape):
    return pl.BlockSpec(shape, lambda b: (0,) * len(shape))


def params():
    return pltpu.CompilerParams(vmem_limit_bytes=VMEM)


def cost(fields, passes, size):
    return pl.CostEstimate(
        flops=int(fields * passes * 2 * 128 * 256 * 256), bytes_accessed=int(size), transcendentals=0
    )


def shards(ensemble, gradient):
    members, levels, rows, width = ensemble.shape
    total = members * levels
    ens = ensemble.reshape(total, rows, width)
    bf = jnp.bfloat16
    n_p = 2
    n_q = 2
    rest = (total - GROUP * (n_p + n_q)) // 4
    p_end = GROUP * n_p
    q_end = p_end + GROUP * n_q
    select, spread, center = lon_constants(width)
    lat = band(rows, EDGE).T.copy()
    select, spread, center, lat = map(jnp.asarray, (select, spread, center, lat))
    select4, spread4 = select[:4], spread[:4]

    def block(n, r, c, shift=0):
        return pl.BlockSpec((n, r, c), lambda b: (b + shift, 0, 0))

    grad_spec = whole(levels, rows, width)
    select_spec = whole(8, width, 2 * LANES)
    spread_spec = whole(8, 2 * LANES, width)
    center_spec = whole(width, width)
    lat_spec = whole(rows, rows + 2 * EDGE)
    tile = block(4, rows, LANES)
    field_bytes = rows * width * 2

    p_right, p_left = pl.pallas_call(
        pack_kernel,
        grid=(n_p,),
        in_specs=[block(GROUP, rows, width), grad_spec, select_spec],
        out_specs=[tile, tile],
        out_shape=[jax.ShapeDtypeStruct((4 * n_p, rows, LANES), bf)] * 2,
        compiler_params=params(),
        cost_estimate=cost(p_end, 1, p_end * field_bytes),
        name="pack_edges",
    )(ens, gradient, select)
    p_low, p_high = exchange(p_right, p_left, "lon", True)

    n_rows = total - p_end
    step = 2
    last = rows // EDGE - 1
    q_up, q_down = pl.pallas_call(
        lambda *refs: rows_kernel(p_end, *refs),
        grid=(n_rows // step,),
        in_specs=[
            pl.BlockSpec((step, EDGE, width), lambda b: (b + p_end // step, 0, 0)),
            pl.BlockSpec((step, EDGE, width), lambda b: (b + p_end // step, last, 0)),
            pl.BlockSpec((levels, EDGE, width), lambda b: (0, 0, 0)),
            pl.BlockSpec((levels, EDGE, width), lambda b: (0, last, 0)),
        ],
        out_specs=[block(step, EDGE, width)] * 2,
        out_shape=[jax.ShapeDtypeStruct((n_rows, EDGE, width), bf)] * 2,
        compiler_params=params(),
        cost_estimate=cost(0, 0, n_rows * field_bytes),
        name="edge_rows",
    )(ens, ens, gradient, gradient)
    q_low, q_high = exchange(q_up, q_down, "lat", False)

    halo = block(GROUP, EDGE, width)
    q_done, q_right, q_left = pl.pallas_call(
        lambda *refs: lat_pack_kernel(p_end, *refs),
        grid=(n_q,),
        in_specs=[block(GROUP, rows, width, n_p), grad_spec, halo, halo, lat_spec, select_spec],
        out_specs=[block(GROUP, rows, width), tile, tile],
        out_shape=[jax.ShapeDtypeStruct((GROUP * n_q, rows, width), bf)]
        + [jax.ShapeDtypeStruct((4 * n_q, rows, LANES), bf)] * 2,
        compiler_params=params(),
        cost_estimate=cost(GROUP * n_q, 3, GROUP * n_q * field_bytes * 2),
        name="lat_then_pack",
    )(ens, gradient, q_low, q_high, lat, select)
    q_in = exchange(q_right, q_left, "lon", True)

    shift = q_end // 4
    halo4 = pl.BlockSpec((4, EDGE, width), lambda b: (b, 0, 0))
    r_done, r_right, r_left = pl.pallas_call(
        lambda *refs: lat_pack4_kernel(q_end, *refs),
        grid=(rest,),
        in_specs=[
            block(4, rows, width, shift),
            grad_spec,
            halo4,
            halo4,
            lat_spec,
            whole(4, width, 2 * LANES),
        ],
        out_specs=[block(4, rows, width), block(1, rows, LANES), block(1, rows, LANES)],
        out_shape=[jax.ShapeDtypeStruct((4 * rest, rows, width), bf)]
        + [jax.ShapeDtypeStruct((rest, rows, LANES), bf)] * 2,
        compiler_params=params(),
        cost_estimate=cost(4 * rest, 3, 4 * rest * field_bytes * 2),
        name="lat_then_pack_rest",
    )(ens, gradient, q_low[GROUP * n_q :], q_high[GROUP * n_q :], lat, select4)
    r_in = exchange(r_right, r_left, "lon", True)

    p_done, p_up, p_down = pl.pallas_call(
        lon_kernel,
        grid=(n_p,),
        in_specs=[block(GROUP, rows, width), grad_spec, tile, tile, center_spec, spread_spec],
        out_specs=[block(GROUP, rows, width), halo, halo],
        out_shape=[jax.ShapeDtypeStruct((p_end, rows, width), bf)]
        + [jax.ShapeDtypeStruct((p_end, EDGE, width), bf)] * 2,
        compiler_params=params(),
        cost_estimate=cost(p_end, 2, p_end * field_bytes * 2),
        name="lon_sums",
    )(ens, gradient, p_low, p_high, center, spread)
    lat_low, lat_high = exchange(p_up, p_down, "lat", False)

    out_shape = jax.ShapeDtypeStruct((total, rows, width), bf)
    out = pl.pallas_call(
        lat_kernel,
        grid=(n_p,),
        in_specs=[block(GROUP, rows, width), halo, halo, lat_spec],
        out_specs=block(GROUP, rows, width),
        out_shape=out_shape,
        compiler_params=params(),
        cost_estimate=cost(p_end, 1, p_end * field_bytes * 2),
        name="lat_sums",
    )(p_done, lat_low, lat_high, lat)

    out = pl.pallas_call(
        last_kernel,
        grid=(n_q,),
        in_specs=[
            block(GROUP, rows, width),
            tile,
            tile,
            center_spec,
            spread_spec,
            pl.BlockSpec(memory_space=pl.ANY),
        ],
        out_specs=block(GROUP, rows, width, n_p),
        out_shape=out_shape,
        input_output_aliases={5: 0},
        compiler_params=params(),
        cost_estimate=cost(GROUP * n_q, 2, GROUP * n_q * field_bytes * 2),
        name="lon_sums_last",
    )(q_done, *q_in, center, spread, out)

    out = pl.pallas_call(
        last4_kernel,
        grid=(rest,),
        in_specs=[
            block(4, rows, width),
            block(1, rows, LANES),
            block(1, rows, LANES),
            center_spec,
            whole(4, 2 * LANES, width),
            pl.BlockSpec(memory_space=pl.ANY),
        ],
        out_specs=block(4, rows, width, shift),
        out_shape=out_shape,
        input_output_aliases={5: 0},
        compiler_params=params(),
        cost_estimate=cost(4 * rest, 2, 4 * rest * field_bytes * 2),
        name="lon_sums_rest",
    )(r_done, *r_in, center, spread4, out)
    return out.reshape(members, levels, rows, width)


def solution(mesh):
    placed = (P(None, None, "lat", "lon"), P(None, "lat", "lon"))
    return jax.shard_map(
        shards, mesh=mesh, in_specs=placed, out_specs=P(None, None, "lat", "lon"), check_vma=False
    )
```

```python
import functools

import jax
import jax.numpy as jnp
import numpy as np
from jax import lax
from jax.experimental import pallas as pl
from jax.experimental.pallas import tpu as pltpu
from jax.sharding import PartitionSpec as P

HALF = 30
LANES = 128
EDGE = 32
GROUP = 17
VMEM_LIMIT = 16 * 1024 * 1024
FIRST = 42
HEAVY = 200_000_000_000
BF = jnp.bfloat16


def taps():
    offsets = np.arange(-HALF, HALF + 1).astype(np.float32)
    spread = np.float32(HALF)
    norm = np.sqrt(np.sum(np.exp(-offsets * offsets / (spread * spread)), dtype=np.float32))
    return (np.exp(-offsets * offsets / (2 * spread * spread)) / norm).astype(BF)


def band(block_len, margin):
    k = taps()
    out = np.zeros((block_len + 2 * margin, block_len), BF)
    for q in range(block_len):
        out[q + margin - HALF : q + margin + HALF + 1, q] = k
    return out


def lon_weights(width):
    lon = band(width, HALF)
    spread = np.zeros((8, 2 * LANES, width), BF)
    for s in range(8):
        for j in range(HALF):
            lane = HALF * s + j if s < 4 else 120 + j - 8 * (s - 4)
            if s >= 4 and not 120 <= lane < 128:
                continue
            spread[s, lane] = lon[j]
            spread[s, LANES + lane] = lon[width + HALF + j]
    return lon[HALF : HALF + width].copy(), spread


def odd(axis):
    return lax.rem(lax.axis_index(axis), 2)


def fill_select(select_ref):
    width = select_ref.shape[1]
    side = odd("lon")
    row = lax.broadcasted_iota(jnp.int32, (width, 2 * LANES), 0)
    col = lax.broadcasted_iota(jnp.int32, (width, 2 * LANES), 1)
    diff = row - col
    end_tile, start_tile = side * LANES, (1 - side) * LANES
    for s in range(8):
        shift, lo, hi = (-HALF * s, HALF * s, HALF * s + HALF) if s < 4 else (8 * (s - 4) - 120, 120, 128)
        end = (diff == width - HALF + shift - end_tile) & (col >= end_tile + lo) & (col < end_tile + hi)
        start = (diff == shift - start_tile) & (col >= start_tile + lo) & (col < start_tile + hi) & (row < HALF)
        select_ref[s] = jnp.where(end | start, 1.0, 0.0).astype(BF)


def dot(a, b):
    return jnp.dot(a, b, preferred_element_type=jnp.float32)


def units(count):
    out, first = [], 0
    while count - first >= GROUP:
        out.append((first, 4, True))
        first += GROUP
    if count > first:
        out.append((first, (count - first) // 4, False))
    return out


def tiles_of(count):
    return sum(t for _, t, _ in units(count))


def stack(ref, first, count):
    return ref[first : first + count].reshape(count * ref.shape[1], ref.shape[2])


def pack(src_ref, unit, select_ref):
    first, n, extra = unit
    rows = src_ref.shape[1]
    acc = None
    for s in range(4):
        part = dot(stack(src_ref, first + s * n, n), select_ref[s])
        acc = part if acc is None else acc + part
    if extra:
        field = src_ref[first + 4 * n]
        acc += jnp.concatenate([dot(field, select_ref[4 + t]) for t in range(n)], axis=0)
    return acc.astype(BF).reshape(n, rows, 2 * LANES)


def multiply(raw_ref, number, gvm_ref, prod_ref):
    for f in range(prod_ref.shape[0]):
        grad = gvm_ref[(number + f) % gvm_ref.shape[0]].astype(jnp.float32)
        prod_ref[f] = (raw_ref[f].astype(jnp.float32) * grad).astype(BF)


def packed_units(src_ref, select_ref):
    tile = 0
    for unit in units(src_ref.shape[0]):
        yield pl.ds(tile, unit[1]), pack(src_ref, unit, select_ref)
        tile += unit[1]


def first_kernel(ens_ref, grad_ref, a_ref, b_ref, prod_ref, select_ref, gvm_ref, buf, sems):
    count = prod_ref.shape[0]
    copies = [
        pltpu.make_async_copy(grad_ref, gvm_ref, sems.at[0]),
        pltpu.make_async_copy(ens_ref.at[pl.ds(0, count)], buf, sems.at[1]),
    ]
    for c in copies:
        c.start()
    fill_select(select_ref)
    for c in copies:
        c.wait()
    multiply(buf, 0, gvm_ref, prod_ref)
    for at, tiles in packed_units(prod_ref, select_ref):
        a_ref[at] = tiles[:, :, :LANES]
        b_ref[at] = tiles[:, :, LANES:]


def edge_rows(ref, rows):
    side = odd("lat")
    head, tail = 0, rows - EDGE
    return (
        pl.ds(pl.multiple_of((1 - side) * tail, EDGE), EDGE),
        pl.ds(pl.multiple_of(side * tail, EDGE), EDGE),
    )


def second_kernel(
    before, ens_ref, gvm_ref, select_ref, b_first_ref, prod_ref, a_ref, b_ref, near_ref, far_ref, buf, sem
):
    count, rows = prod_ref.shape[:2]
    copy = pltpu.make_async_copy(ens_ref.at[pl.ds(before, count)], buf, sem)
    copy.start()
    copy.wait()
    multiply(buf, before, gvm_ref, prod_ref)
    for at, tiles in packed_units(prod_ref, select_ref):
        a_ref[at] = tiles[:, :, :LANES]
        b_ref[at] = tiles[:, :, LANES:]
    near, far = edge_rows(b_ref, rows)
    start = 0
    for ref in (b_first_ref, b_ref):
        to = pl.ds(start, ref.shape[0])
        near_ref[to] = ref[:, near]
        far_ref[to] = ref[:, far]
        start += ref.shape[0]


def pair(ref, t):
    if t + 1 < ref.shape[0]:
        return jnp.concatenate([ref[t], ref[t + 1]], axis=1)
    return ref[t]


def lat_field(field, near, far, lat):
    return dot(lat, jnp.concatenate([near, field, far], axis=0))


def lat_tiles(refs, near_ref, far_ref, lat, emit):
    start = 0
    for ref in refs:
        for t in range(0, ref.shape[0], 2):
            n = min(2, ref.shape[0] - t)
            wide = [jnp.concatenate([r[start + t + i] for i in range(n)], axis=1) for r in (near_ref, far_ref)]
            done = lat_field(pair(ref, t), *wide, lat).astype(BF)
            for i in range(n):
                emit(start + t + i, done[:, i * LANES : (i + 1) * LANES])
        start += ref.shape[0]


def edge_lat_kernel(one_ref, two_ref, near_ref, far_ref, lat_ref, out_ref):
    def emit(t, v):
        out_ref[t] = v

    lat_tiles((one_ref, two_ref), near_ref, far_ref, lat_ref[odd("lat")], emit)


def own_kernel(one_ref, two_ref, center_ref, own_ref, near_ref, far_ref):
    rows, width = own_ref.shape[1:]
    start = 0
    for prod_ref in (one_ref, two_ref):
        count = prod_ref.shape[0]
        for first in range(0, count, 4):
            n = min(4, count - first)
            v = dot(stack(prod_ref, first, n), center_ref[...]).astype(BF).reshape(n, rows, width)
            own_ref[pl.ds(start + first, n)] = v
        start += count
    near, far = edge_rows(own_ref, rows)
    near_ref[...] = own_ref[:, near]
    far_ref[...] = own_ref[:, far]


def tile_rows_kernel(one_ref, two_ref, near_ref, far_ref):
    near, far = edge_rows(one_ref, one_ref.shape[1])
    start = 0
    for ref in (one_ref, two_ref):
        to = pl.ds(start, ref.shape[0])
        near_ref[to] = ref[:, near]
        far_ref[to] = ref[:, far]
        start += ref.shape[0]


def spread_rows(first):
    side = odd("lon") if first else 1 - odd("lon")
    return pl.ds(pl.multiple_of((1 - side) * LANES, LANES), LANES)


def partial_kernel(
    counts, own_ref, near_ref, far_ref, one_ref, two_ref, tnear_ref, tfar_ref, lat_ref, spread_ref, acc_ref, done
):
    lat = lat_ref[odd("lat")]
    rows, width = own_ref.shape[1:]
    at = spread_rows(True)

    def emit(t, v):
        done[t] = v

    lat_tiles((one_ref, two_ref), tnear_ref, tfar_ref, lat, emit)

    def own(first, n):
        return jnp.concatenate(
            [lat_field(own_ref[f], near_ref[f], far_ref[f], lat) for f in range(first, first + n)], axis=0
        )

    for first, n, extra, tile in all_units(counts):
        edges = stack(done, tile, n)
        for s in range(4):
            v = own(first + s * n, n) + dot(edges, spread_ref[s, at])
            acc_ref[pl.ds(first + s * n, n)] = v.reshape(n, rows, width)
        if extra:
            v = own(first + 4 * n, 1)
            for t in range(n):
                v += dot(done[tile + t], spread_ref[4 + t, at])
            acc_ref[first + 4 * n] = v


def last_kernel(counts, acc_ref, tiles_ref, spread_ref, out_ref, buf, sems):
    rows, width = acc_ref.shape[1:]
    at = spread_rows(False)
    copies = []
    for first, n, extra, tile in all_units(counts):
        edges = stack(tiles_ref, tile, n)
        for s in range(4):
            to = pl.ds(first + s * n, n)
            buf[to] = (acc_ref[to] + dot(edges, spread_ref[s, at]).reshape(n, rows, width)).astype(BF)
        if extra:
            v = acc_ref[first + 4 * n]
            for t in range(n):
                v += dot(tiles_ref[tile + t], spread_ref[4 + t, at])
            buf[first + 4 * n] = v.astype(BF)
        to = pl.ds(first, 4 * n + extra)
        copies.append(pltpu.make_async_copy(buf.at[to], out_ref.at[to], sems.at[len(copies)]))
        copies[-1].start()
    for c in copies:
        c.wait()


def all_units(counts):
    out, start, tile = [], 0, 0
    for count in counts:
        for first, n, extra in units(count):
            out.append((start + first, n, extra, tile))
            tile += n
        start += count
    return out


def first_partner(x, axis):
    return lax.ppermute(x, axis, [(i, i ^ 1) for i in range(lax.axis_size(axis))])


def second_partner(x, axis, periodic):
    count = lax.axis_size(axis)
    pairs = []
    for i in range(count):
        j = i + 1 if i % 2 else i - 1
        if periodic or 0 <= j < count:
            pairs.append((i, j % count))
    return lax.ppermute(x, axis, pairs)


def lat_exchange(near, far):
    return first_partner(near, "lat"), second_partner(far, "lat", False)


IN_VMEM = pl.BlockSpec(memory_space=pltpu.VMEM)
ANYWHERE = pl.BlockSpec(memory_space=pl.ANY)


def vm(x):
    return pltpu.with_memory_space_constraint(x, pltpu.VMEM)


def hbm(x):
    return pltpu.with_memory_space_constraint(x, pltpu.HBM)


def call(kernel, name, args, outs, scratch=(), specs=None, out_specs=None, aliases=None, weight=0):
    return pl.pallas_call(
        kernel,
        in_specs=specs or [IN_VMEM] * len(args),
        out_specs=out_specs or [IN_VMEM] * len(outs),
        out_shape=outs,
        scratch_shapes=list(scratch),
        input_output_aliases=aliases or {},
        compiler_params=pltpu.CompilerParams(vmem_limit_bytes=VMEM_LIMIT),
        cost_estimate=pl.CostEstimate(flops=weight, bytes_accessed=weight, transcendentals=0),
        name=name,
    )(*[vm(a) if specs is None or specs[i] is IN_VMEM else a for i, a in enumerate(args)])


def shards(ensemble, gradient):
    members, levels, rows, width = ensemble.shape
    total = members * levels
    ens = hbm(ensemble.reshape(total, rows, width))
    counts = (FIRST, total - FIRST)
    t_one, t_two = map(tiles_of, counts)
    n_tiles = t_one + t_two
    center, spread = map(jnp.asarray, lon_weights(width))
    low, own, high = np.split(band(rows, EDGE).T, [EDGE, EDGE + rows], axis=1)
    lat = jnp.asarray(np.stack([np.concatenate(v, axis=1) for v in ((high, own, low), (low, own, high))]))

    def shape(n, r=rows, c=width):
        return pltpu.VMEM((n, r, c), BF)

    def tiles(n, r=rows):
        return shape(n, r, LANES)

    dma = pltpu.SemaphoreType.DMA
    a_one, b_one, prod_one, select, grad = call(
        first_kernel,
        "pack_first",
        (ens, hbm(gradient)),
        [tiles(t_one), tiles(t_one), shape(counts[0]), shape(8, width, 2 * LANES), shape(levels)],
        scratch=[shape(counts[0]), dma((2,))],
        specs=[ANYWHERE] * 2,
    )
    a_one = first_partner(a_one, "lon")

    prod_two, a_two, b_two, near, far = call(
        functools.partial(second_kernel, counts[0]),
        "pack_second",
        (ens, grad, select, b_one),
        [shape(counts[1]), tiles(t_two), tiles(t_two), tiles(n_tiles, EDGE), tiles(n_tiles, EDGE)],
        scratch=[shape(counts[1]), dma],
        specs=[ANYWHERE, IN_VMEM, IN_VMEM, IN_VMEM],
    )
    a_two = first_partner(a_two, "lon")
    near, far = lat_exchange(near, far)
    (b,) = call(edge_lat_kernel, "edge_lat_sums", (b_one, b_two, near, far, lat), [tiles(n_tiles)])
    b = second_partner(b, "lon", True)

    own, near, far = call(
        own_kernel, "own_lon_sums", (prod_one, prod_two, center), [shape(total)] + [shape(total, EDGE)] * 2
    )
    near, far = lat_exchange(near, far)
    tnear, tfar = call(
        tile_rows_kernel, "tile_rows", (a_one, a_two), [tiles(n_tiles, EDGE)] * 2, weight=HEAVY
    )
    tnear, tfar = lat_exchange(tnear, tfar)
    (acc,) = call(
        functools.partial(partial_kernel, counts),
        "all_but_second",
        (own, near, far, a_one, a_two, tnear, tfar, lat, spread),
        [pltpu.VMEM((total, rows, width), jnp.float32)],
        scratch=[tiles(n_tiles)],
    )
    (result,) = call(
        functools.partial(last_kernel, counts),
        "add_second",
        (acc, b, spread),
        [jax.ShapeDtypeStruct((total, rows, width), BF)],
        scratch=[shape(total), dma((len(all_units(counts)),))],
        out_specs=[ANYWHERE],
    )
    return result.reshape(members, levels, rows, width)


def solution(mesh):
    placed = (P(None, None, "lat", "lon"), P(None, "lat", "lon"))
    return jax.shard_map(
        shards, mesh=mesh, in_specs=placed, out_specs=P(None, None, "lat", "lon"), check_vma=False
    )
```

```python
import functools

import jax
import jax.numpy as jnp
import numpy as np
from jax import lax
from jax.experimental import pallas as pl
from jax.experimental.pallas import tpu as pltpu
from jax.sharding import PartitionSpec as P

HALF = 30
LANES = 128
EDGE = 32
GROUP = 17
VMEM_LIMIT = 16 * 1024 * 1024
FIRST = 42
LAST = 2
BATCH = 8
HEAVY = 10_000_000_000
BF = jnp.bfloat16


def taps():
    offsets = np.arange(-HALF, HALF + 1).astype(np.float32)
    spread = np.float32(HALF)
    norm = np.sqrt(np.sum(np.exp(-offsets * offsets / (spread * spread)), dtype=np.float32))
    return (np.exp(-offsets * offsets / (2 * spread * spread)) / norm).astype(BF)


def band(block_len, margin):
    k = taps()
    out = np.zeros((block_len + 2 * margin, block_len), BF)
    for q in range(block_len):
        out[q + margin - HALF : q + margin + HALF + 1, q] = k
    return out


def lon_weights(width):
    lon = band(width, HALF)
    spread = np.zeros((8, 2 * LANES, width), BF)
    for s in range(8):
        for j in range(HALF):
            lane = HALF * s + j if s < 4 else 120 + j - 8 * (s - 4)
            if s >= 4 and not 120 <= lane < 128:
                continue
            spread[s, lane] = lon[j]
            spread[s, LANES + lane] = lon[width + HALF + j]
    return lon[HALF : HALF + width].copy(), spread


def odd(axis):
    return lax.rem(lax.axis_index(axis), 2)


def fill_select(select_ref):
    width = select_ref.shape[1]
    side = odd("lon")
    row = lax.broadcasted_iota(jnp.int32, (width, 2 * LANES), 0)
    col = lax.broadcasted_iota(jnp.int32, (width, 2 * LANES), 1)
    diff = row - col
    end_tile, start_tile = side * LANES, (1 - side) * LANES
    for s in range(8):
        shift, lo, hi = (-HALF * s, HALF * s, HALF * s + HALF) if s < 4 else (8 * (s - 4) - 120, 120, 128)
        end = (diff == width - HALF + shift - end_tile) & (col >= end_tile + lo) & (col < end_tile + hi)
        start = (diff == shift - start_tile) & (col >= start_tile + lo) & (col < start_tile + hi) & (row < HALF)
        select_ref[s] = jnp.where(end | start, 1.0, 0.0).astype(BF)


def dot(a, b):
    return jnp.dot(a, b, preferred_element_type=jnp.float32)


def units(count):
    out, first = [], 0
    while count - first >= GROUP:
        out.append((first, 4, True))
        first += GROUP
    if count > first:
        out.append((first, (count - first) // 4, False))
    return out


def tiles_of(count):
    return sum(t for _, t, _ in units(count))


def stack(ref, first, count):
    return ref[first : first + count].reshape(count * ref.shape[1], ref.shape[2])


def pack(src_ref, unit, select_ref):
    first, n, extra = unit
    rows = src_ref.shape[1]
    acc = None
    for s in range(4):
        part = dot(stack(src_ref, first + s * n, n), select_ref[s])
        acc = part if acc is None else acc + part
    if extra:
        field = src_ref[first + 4 * n]
        acc += jnp.concatenate([dot(field, select_ref[4 + t]) for t in range(n)], axis=0)
    return acc.astype(BF).reshape(n, rows, 2 * LANES)


def multiply(raw_ref, number, gvm_ref, prod_ref):
    for f in range(prod_ref.shape[0]):
        grad = gvm_ref[(number + f) % gvm_ref.shape[0]].astype(jnp.float32)
        prod_ref[f] = (raw_ref[f].astype(jnp.float32) * grad).astype(BF)


def packed_units(src_ref, select_ref):
    tile = 0
    for unit in units(src_ref.shape[0]):
        yield pl.ds(tile, unit[1]), pack(src_ref, unit, select_ref)
        tile += unit[1]


def first_kernel(ens_ref, grad_ref, a_ref, b_ref, prod_ref, select_ref, gvm_ref, buf, sems):
    count = prod_ref.shape[0]
    copies = [
        pltpu.make_async_copy(grad_ref, gvm_ref, sems.at[0]),
        pltpu.make_async_copy(ens_ref.at[pl.ds(0, count)], buf, sems.at[1]),
    ]
    for c in copies:
        c.start()
    fill_select(select_ref)
    for c in copies:
        c.wait()
    multiply(buf, 0, gvm_ref, prod_ref)
    for at, tiles in packed_units(prod_ref, select_ref):
        a_ref[at] = tiles[:, :, :LANES]
        b_ref[at] = tiles[:, :, LANES:]


def emit_rows(v, near_ref, far_ref, at):
    up = odd("lat") == 0
    head, tail = v[:, :EDGE], v[:, v.shape[1] - EDGE :]
    near_ref[at] = jnp.where(up, tail, head)
    far_ref[at] = jnp.where(up, head, tail)


def second_kernel(
    before, ens_ref, gvm_ref, select_ref, b_first_ref, prod_ref, a_ref, b_ref, near_ref, far_ref, buf, sem
):
    count = prod_ref.shape[0]
    copy = pltpu.make_async_copy(ens_ref.at[pl.ds(before, count)], buf, sem)
    copy.start()
    skip = b_first_ref.shape[0]
    for t in range(skip):
        emit_rows(b_first_ref[t : t + 1], near_ref, far_ref, pl.ds(t, 1))
    copy.wait()
    multiply(buf, before, gvm_ref, prod_ref)
    for at, tiles in packed_units(prod_ref, select_ref):
        a_ref[at] = tiles[:, :, :LANES]
        b_ref[at] = tiles[:, :, LANES:]
        emit_rows(tiles[:, :, LANES:], near_ref, far_ref, pl.ds(skip + at.start, at.size))


def rows_kernel(one_ref, two_ref, near_ref, far_ref):
    start = 0
    for ref in (one_ref, two_ref):
        for f in range(0, ref.shape[0], 4):
            n = min(4, ref.shape[0] - f)
            emit_rows(ref[f : f + n], near_ref, far_ref, pl.ds(start + f, n))
        start += ref.shape[0]


def lat_field(field, low, high, lat_ref):
    return dot(lat_ref[...], jnp.concatenate([low, field, high], axis=0))


def lat_tiles(refs, near_ref, far_ref, order, lat_ref, emit):
    start = 0
    for ref in refs:
        for t in range(0, ref.shape[0], 2):
            n = min(2, ref.shape[0] - t)
            wide = [
                jnp.concatenate([r[i] for i in range(first, first + n)], axis=1)
                for r, first in ((ref, t), (near_ref, start + t), (far_ref, start + t))
            ]
            done = lat_field(wide[0], *order(*wide[1:]), lat_ref).astype(BF)
            for i in range(n):
                emit(start + t + i, done[:, i * LANES : (i + 1) * LANES])
        start += ref.shape[0]


def edge_lat_kernel(one_ref, two_ref, near_ref, far_ref, lat_ref, *refs):
    up = odd("lat") == 0
    out_refs = [r for r in refs if r.shape[1:] == one_ref.shape[1:]]

    def order(near, far):
        return jnp.where(up, far, near), jnp.where(up, near, far)

    def emit(t, v):
        for ref in out_refs:
            if t < ref.shape[0]:
                ref[t] = v
                return
            t -= ref.shape[0]

    lat_tiles((one_ref, two_ref), near_ref, far_ref, order, lat_ref, emit)


def add_rows(acc_ref, rows_ref, start, near, center_ref, border_ref):
    low = odd("lat") if near else 1 - odd("lat")
    edge = acc_ref.shape[1] - EDGE
    at = pl.ds(pl.multiple_of((1 - low) * edge, EDGE), EDGE)
    for first in range(0, acc_ref.shape[0], BATCH):
        count = min(BATCH, acc_ref.shape[0] - first)
        own = dot(stack(rows_ref, start + first, count), center_ref[...]).astype(BF)
        part = dot(border_ref[low, : count * EDGE, : count * EDGE], own)
        for i in range(count):
            acc_ref[first + i, at] += part[i * EDGE : (i + 1) * EDGE]


def tile_rows_kernel(one_ref, two_ref, after_ref, near_ref, far_ref):
    del after_ref
    rows_kernel(one_ref, two_ref, near_ref, far_ref)


def own_kernel(one_ref, two_ref, center_ref, lat_ref, acc_ref):
    rows, width = acc_ref.shape[1:]
    start = 0
    for ref in (one_ref, two_ref):
        for f in range(0, ref.shape[0], 4):
            n = min(4, ref.shape[0] - f)
            own = dot(stack(ref, f, n), center_ref[...]).astype(BF)
            for i in range(n):
                acc_ref[start + f + i] = dot(lat_ref[:, EDGE : EDGE + rows], own[i * rows : (i + 1) * rows])
        start += ref.shape[0]


def halo_kernel(own_ref, near_ref, far_ref, center_ref, border_ref, acc_ref):
    del own_ref
    add_rows(acc_ref, near_ref, 0, True, center_ref, border_ref)
    add_rows(acc_ref, far_ref, 0, False, center_ref, border_ref)


def last_kernel(plan, acc_ref, done_ref, tiles_ref, spread_ref, *refs):
    out_ref, buf, sems = refs[-3:]
    rows, width = acc_ref.shape[1:]
    up = odd("lon") == 0
    start, skip = plan[0][0], plan[0][3]
    copies = []
    for first, n, extra, tile in plan:
        a, b = stack(done_ref, tile, n), stack(tiles_ref, tile - skip, n)
        edges = jnp.concatenate([jnp.where(up, b, a), jnp.where(up, a, b)], axis=1)
        for s in range(4):
            at = pl.ds(first + s * n, n)
            v = acc_ref[at] + dot(edges, spread_ref[s]).reshape(n, rows, width)
            buf[pl.ds(first - start + s * n, n)] = v.astype(BF)
        if extra:
            v = acc_ref[first + 4 * n]
            for t in range(n):
                v += dot(edges[t * rows : (t + 1) * rows], spread_ref[4 + t])
            buf[first - start + 4 * n] = v.astype(BF)
        count = 4 * n + extra
        from_, to = pl.ds(first - start, count), pl.ds(first, count)
        copies.append(pltpu.make_async_copy(buf.at[from_], out_ref.at[to], sems.at[len(copies)]))
        copies[-1].start()
    for c in copies:
        c.wait()


def all_units(counts):
    out, start, tile = [], 0, 0
    for count in counts:
        for first, n, extra in units(count):
            out.append((start + first, n, extra, tile))
            tile += n
        start += count
    return out


def first_partner(x, axis):
    return lax.ppermute(x, axis, [(i, i ^ 1) for i in range(lax.axis_size(axis))])


def second_partner(x, axis, periodic):
    count = lax.axis_size(axis)
    pairs = []
    for i in range(count):
        j = i + 1 if i % 2 else i - 1
        if periodic or 0 <= j < count:
            pairs.append((i, j % count))
    return lax.ppermute(x, axis, pairs)


def lat_exchange(near, far):
    return first_partner(near, "lat"), second_partner(far, "lat", False)


IN_VMEM = pl.BlockSpec(memory_space=pltpu.VMEM)
ANYWHERE = pl.BlockSpec(memory_space=pl.ANY)


def vm(x):
    return pltpu.with_memory_space_constraint(x, pltpu.VMEM)


def hbm(x):
    return pltpu.with_memory_space_constraint(x, pltpu.HBM)


def call(kernel, name, args, outs, scratch=(), specs=None, out_specs=None, aliases=None, weight=0):
    return pl.pallas_call(
        kernel,
        in_specs=specs or [IN_VMEM] * len(args),
        out_specs=out_specs or [IN_VMEM] * len(outs),
        out_shape=outs,
        scratch_shapes=list(scratch),
        input_output_aliases=aliases or {},
        compiler_params=pltpu.CompilerParams(vmem_limit_bytes=VMEM_LIMIT),
        cost_estimate=pl.CostEstimate(flops=weight, bytes_accessed=weight, transcendentals=0),
        name=name,
    )(*[vm(a) if specs is None or specs[i] is IN_VMEM else a for i, a in enumerate(args)])


def shards(ensemble, gradient):
    members, levels, rows, width = ensemble.shape
    total = members * levels
    ens = hbm(ensemble.reshape(total, rows, width))
    counts = (FIRST, total - FIRST)
    t_one, t_two = map(tiles_of, counts)
    n_tiles = t_one + t_two
    center, spread = map(jnp.asarray, lon_weights(width))
    lat = band(rows, EDGE).T
    eye = np.eye(BATCH)
    border = jnp.asarray(
        np.stack([np.kron(eye, lat[rows - EDGE :, rows + EDGE :]), np.kron(eye, lat[:EDGE, :EDGE])]).astype(BF)
    )
    lat = jnp.asarray(lat.copy())

    def shape(n, r=rows, c=width):
        return pltpu.VMEM((n, r, c), BF)

    def tiles(n, r=rows):
        return shape(n, r, LANES)

    dma = pltpu.SemaphoreType.DMA
    a_one, b_one, prod_one, select, grad = call(
        first_kernel,
        "pack_first",
        (ens, hbm(gradient)),
        [tiles(t_one), tiles(t_one), shape(counts[0]), shape(8, width, 2 * LANES), shape(levels)],
        scratch=[shape(counts[0]), dma((2,))],
        specs=[ANYWHERE] * 2,
    )
    a_one = first_partner(a_one, "lon")

    prod_two, a_two, b_two, near, far = call(
        functools.partial(second_kernel, counts[0]),
        "pack_second",
        (ens, grad, select, b_one),
        [shape(counts[1]), tiles(t_two), tiles(t_two), tiles(n_tiles, EDGE), tiles(n_tiles, EDGE)],
        scratch=[shape(counts[1]), dma],
        specs=[ANYWHERE, IN_VMEM, IN_VMEM, IN_VMEM],
    )
    a_two = first_partner(a_two, "lon")
    tnear, tfar = lat_exchange(near, far)
    near, far = call(rows_kernel, "edge_rows", (prod_one, prod_two), [shape(total, EDGE)] * 2)
    near, far = lat_exchange(near, far)
    sums = pltpu.VMEM((total, rows, width), jnp.float32)
    (acc,) = call(own_kernel, "own_sums", (prod_one, prod_two, center, lat), [sums])
    plan = all_units(counts)
    t_last = sum(n for _, n, _, _ in plan[-LAST:])
    payload, payload_last = call(
        edge_lat_kernel,
        "edge_lat_sums",
        (b_one, b_two, tnear, tfar, lat, acc),
        [tiles(n_tiles - t_last), tiles(t_last)],
    )
    b = second_partner(payload, "lon", True)

    tnear, tfar = call(
        tile_rows_kernel, "tile_rows", (a_one, a_two, acc), [tiles(n_tiles, EDGE)] * 2, weight=HEAVY
    )
    tnear, tfar = lat_exchange(tnear, tfar)
    b_last = second_partner(payload_last, "lon", True)
    (acc,) = call(halo_kernel, "halo_rows", (acc, near, far, center, border), [sums], aliases={0: 0})
    (done,) = call(edge_lat_kernel, "first_lat_sums", (a_one, a_two, tnear, tfar, lat), [tiles(n_tiles)])

    def finish(part, tiles_in, whole, name):
        args = (acc, done, tiles_in, spread, *whole)
        (result,) = call(
            functools.partial(last_kernel, part),
            name,
            args,
            [jax.ShapeDtypeStruct((total, rows, width), BF)],
            scratch=[shape(sum(4 * n + x for _, n, x, _ in part)), dma((len(part),))],
            specs=[IN_VMEM] * 4 + [ANYWHERE] * len(whole),
            out_specs=[ANYWHERE],
            aliases={4: 0} if whole else None,
        )
        return result

    result = finish(plan[:-LAST], b, (), "edge_sums")
    result = finish(plan[-LAST:], b_last, (result,), "edge_sums_last")
    return result.reshape(members, levels, rows, width)


def solution(mesh):
    placed = (P(None, None, "lat", "lon"), P(None, "lat", "lon"))
    return jax.shard_map(
        shards, mesh=mesh, in_specs=placed, out_specs=P(None, None, "lat", "lon"), check_vma=False
    )
```

```python
import functools

import jax
import jax.numpy as jnp
import numpy as np
from jax import lax
from jax.experimental import pallas as pl
from jax.experimental.pallas import tpu as pltpu
from jax.sharding import PartitionSpec as P

HALF = 30
LANES = 128
EDGE = 32
GROUP = 17
VMEM_LIMIT = 16 * 1024 * 1024
CHUNKS = (46, 34)
BATCH = 8
HEAVY = 25_000_000_000
BF = jnp.bfloat16


def taps():
    offsets = np.arange(-HALF, HALF + 1).astype(np.float32)
    spread = np.float32(HALF)
    norm = np.sqrt(np.sum(np.exp(-offsets * offsets / (spread * spread)), dtype=np.float32))
    return (np.exp(-offsets * offsets / (2 * spread * spread)) / norm).astype(BF)


def band(block_len, margin):
    k = taps()
    out = np.zeros((block_len + 2 * margin, block_len), BF)
    for q in range(block_len):
        out[q + margin - HALF : q + margin + HALF + 1, q] = k
    return out


def lon_weights(width):
    lon = band(width, HALF)
    spread = np.zeros((8, 2 * LANES, width), BF)
    for s in range(8):
        for j in range(HALF):
            lane = HALF * s + j if s < 4 else 120 + j - 8 * (s - 4)
            if s >= 4 and not 120 <= lane < 128:
                continue
            spread[s, lane] = lon[j]
            spread[s, LANES + lane] = lon[width + HALF + j]
    return lon[HALF : HALF + width].copy(), spread


def odd(axis):
    return lax.rem(lax.axis_index(axis), 2)


def fill_select(select_ref):
    width = select_ref.shape[1]
    side = odd("lon")
    row = lax.broadcasted_iota(jnp.int32, (width, 2 * LANES), 0)
    col = lax.broadcasted_iota(jnp.int32, (width, 2 * LANES), 1)
    diff = row - col
    end_tile, start_tile = side * LANES, (1 - side) * LANES
    for s in range(8):
        shift, lo, hi = (-HALF * s, HALF * s, HALF * s + HALF) if s < 4 else (8 * (s - 4) - 120, 120, 128)
        end = (diff == width - HALF + shift - end_tile) & (col >= end_tile + lo) & (col < end_tile + hi)
        start = (diff == shift - start_tile) & (col >= start_tile + lo) & (col < start_tile + hi) & (row < HALF)
        select_ref[s] = jnp.where(end | start, 1.0, 0.0).astype(BF)


def dot(a, b):
    return jnp.dot(a, b, preferred_element_type=jnp.float32)


def units(count):
    out, first = [], 0
    while count - first >= GROUP:
        out.append((first, 4, True))
        first += GROUP
    if count > first:
        out.append((first, (count - first) // 4, False))
    return out


def tiles_of(count):
    return sum(t for _, t, _ in units(count))


def stack(ref, first, count):
    return ref[first : first + count].reshape(count * ref.shape[1], ref.shape[2])


def pack(src_ref, unit, select_ref):
    first, n, extra = unit
    rows = src_ref.shape[1]
    acc = None
    for s in range(4):
        part = dot(stack(src_ref, first + s * n, n), select_ref[s])
        acc = part if acc is None else acc + part
    if extra:
        field = src_ref[first + 4 * n]
        acc += jnp.concatenate([dot(field, select_ref[4 + t]) for t in range(n)], axis=0)
    return acc.astype(BF).reshape(n, rows, 2 * LANES)


def multiply(raw_ref, start, gvm_ref, prod_ref, count):
    for f in range(start, start + count):
        grad = gvm_ref[f % gvm_ref.shape[0]].astype(jnp.float32)
        prod_ref[f] = (raw_ref[f].astype(jnp.float32) * grad).astype(BF)


def first_kernel(
    ens_ref, grad_ref, edge_ref, inner_ref, b_ref, near_ref, far_ref, prod_ref, gvm_ref, select_ref, buf, sems
):
    grad = pltpu.make_async_copy(grad_ref, gvm_ref, sems.at[0])
    grad.start()
    copies = []
    start = 0
    for i, count in enumerate(CHUNKS):
        at = pl.ds(start, count)
        copies.append(pltpu.make_async_copy(ens_ref.at[at], buf.at[at], sems.at[1 + i]))
        copies[-1].start()
        start += count
    fill_select(select_ref)
    grad.wait()
    start = 0
    rows = prod_ref.shape[1]
    plan = all_units(CHUNKS)
    for copy, count in zip(copies, CHUNKS):
        copy.wait()
        multiply(buf, start, gvm_ref, prod_ref, count)
        for first, n, extra, tile in plan:
            if start <= first < start + count:
                tiles = pack(prod_ref, (first, n, extra), select_ref)
                at = pl.ds(tile, n)
                edge_ref[at, :EDGE] = tiles[:, :EDGE, :LANES]
                edge_ref[at, EDGE:] = tiles[:, rows - EDGE :, :LANES]
                inner_ref[at] = tiles[:, EDGE : rows - EDGE, :LANES]
                b_ref[at] = tiles[:, :, LANES:]
                emit_rows(tiles[:, :, LANES:], near_ref, far_ref, at)
        start += count


def emit_rows(v, near_ref, far_ref, at):
    up = odd("lat") == 0
    head, tail = v[:, :EDGE], v[:, v.shape[1] - EDGE :]
    near_ref[at] = jnp.where(up, tail, head)
    far_ref[at] = jnp.where(up, head, tail)


def rows_kernel(ref, *refs):
    near_ref, far_ref = refs[-2:]
    for f in range(0, ref.shape[0], 4):
        n = min(4, ref.shape[0] - f)
        emit_rows(ref[f : f + n], near_ref, far_ref, pl.ds(f, n))


def lat_field(field, low, high, lat_ref):
    return dot(lat_ref[...], jnp.concatenate([low, field, high], axis=0))


def lat_tiles(count, tile, near_ref, far_ref, lat_ref, out_ref):
    up = odd("lat") == 0
    for t in range(0, count, 2):
        n = min(2, count - t)
        field = jnp.concatenate([tile(i) for i in range(t, t + n)], axis=1)
        near, far = (jnp.concatenate([r[i] for i in range(t, t + n)], axis=1) for r in (near_ref, far_ref))
        done = lat_field(field, jnp.where(up, far, near), jnp.where(up, near, far), lat_ref).astype(BF)
        for i in range(n):
            out_ref[t + i] = done[:, i * LANES : (i + 1) * LANES]


def edge_lat_kernel(tiles_ref, near_ref, far_ref, lat_ref, after_ref, out_ref):
    del after_ref
    lat_tiles(tiles_ref.shape[0], lambda t: tiles_ref[t], near_ref, far_ref, lat_ref, out_ref)


def split_lat_kernel(edge_ref, inner_ref, near_ref, far_ref, lat_ref, after_ref, out_ref):
    del after_ref

    def tile(t):
        return jnp.concatenate([edge_ref[t, :EDGE], inner_ref[t], edge_ref[t, EDGE:]], axis=0)

    lat_tiles(edge_ref.shape[0], tile, near_ref, far_ref, lat_ref, out_ref)


def add_rows(acc_ref, start, total, rows_ref, near, center_ref, border_ref):
    low = odd("lat") if near else 1 - odd("lat")
    edge = acc_ref.shape[1] - EDGE
    at = pl.ds(pl.multiple_of((1 - low) * edge, EDGE), EDGE)
    for first in range(start, start + total, BATCH):
        count = min(BATCH, start + total - first)
        own = dot(stack(rows_ref, first, count), center_ref[...]).astype(BF)
        part = dot(border_ref[low, : count * EDGE, : count * EDGE], own)
        for i in range(count):
            acc_ref[first + i, at] += part[i * EDGE : (i + 1) * EDGE]


def own_kernel(prod_ref, center_ref, lat_ref, after_ref, acc_ref):
    del after_ref
    rows = acc_ref.shape[1]
    for f in range(0, prod_ref.shape[0], 4):
        n = min(4, prod_ref.shape[0] - f)
        own = dot(stack(prod_ref, f, n), center_ref[...]).astype(BF)
        for i in range(n):
            acc_ref[f + i] = dot(lat_ref[:, EDGE : EDGE + rows], own[i * rows : (i + 1) * rows])


def partner_kernel(near, own_ref, rows_ref, center_ref, border_ref, acc_ref):
    del own_ref
    add_rows(acc_ref, 0, acc_ref.shape[0], rows_ref, near, center_ref, border_ref)


def last_kernel(plan, acc_ref, done_ref, tiles_ref, spread_ref, *refs):
    out_ref, buf, sems = refs[-3:]
    rows, width = acc_ref.shape[1:]
    up = odd("lon") == 0
    start, skip = plan[0][0], plan[0][3]
    copies = []
    for first, n, extra, tile in plan:
        a, b = stack(done_ref, tile, n), stack(tiles_ref, tile - skip, n)
        edges = jnp.concatenate([jnp.where(up, b, a), jnp.where(up, a, b)], axis=1)
        for s in range(4):
            at = pl.ds(first + s * n, n)
            v = acc_ref[at] + dot(edges, spread_ref[s]).reshape(n, rows, width)
            buf[pl.ds(first - start + s * n, n)] = v.astype(BF)
        if extra:
            v = acc_ref[first + 4 * n]
            for t in range(n):
                v += dot(edges[t * rows : (t + 1) * rows], spread_ref[4 + t])
            buf[first - start + 4 * n] = v.astype(BF)
        count = 4 * n + extra
        from_, to = pl.ds(first - start, count), pl.ds(first, count)
        copies.append(pltpu.make_async_copy(buf.at[from_], out_ref.at[to], sems.at[len(copies)]))
        copies[-1].start()
    for c in copies:
        c.wait()


def all_units(counts):
    out, start, tile = [], 0, 0
    for count in counts:
        for first, n, extra in units(count):
            out.append((start + first, n, extra, tile))
            tile += n
        start += count
    return out


def first_partner(x, axis):
    return lax.ppermute(x, axis, [(i, i ^ 1) for i in range(lax.axis_size(axis))])


def second_partner(x, axis, periodic):
    count = lax.axis_size(axis)
    pairs = []
    for i in range(count):
        j = i + 1 if i % 2 else i - 1
        if periodic or 0 <= j < count:
            pairs.append((i, j % count))
    return lax.ppermute(x, axis, pairs)


def lat_exchange(near, far):
    return first_partner(near, "lat"), second_partner(far, "lat", False)


IN_VMEM = pl.BlockSpec(memory_space=pltpu.VMEM)
ANYWHERE = pl.BlockSpec(memory_space=pl.ANY)


def vm(x):
    return pltpu.with_memory_space_constraint(x, pltpu.VMEM)


def hbm(x):
    return pltpu.with_memory_space_constraint(x, pltpu.HBM)


def call(kernel, name, args, outs, scratch=(), specs=None, out_specs=None, aliases=None, weight=0):
    return pl.pallas_call(
        kernel,
        in_specs=specs or [IN_VMEM] * len(args),
        out_specs=out_specs or [IN_VMEM] * len(outs),
        out_shape=outs,
        scratch_shapes=list(scratch),
        input_output_aliases=aliases or {},
        compiler_params=pltpu.CompilerParams(vmem_limit_bytes=VMEM_LIMIT),
        cost_estimate=pl.CostEstimate(flops=weight, bytes_accessed=weight, transcendentals=0),
        name=name,
    )(*[vm(a) if specs is None or specs[i] is IN_VMEM else a for i, a in enumerate(args)])


def shards(ensemble, gradient):
    members, levels, rows, width = ensemble.shape
    total = members * levels
    ens = hbm(ensemble.reshape(total, rows, width))
    plan = all_units(CHUNKS)
    n_tiles = sum(n for _, n, _, _ in plan)
    center, spread = map(jnp.asarray, lon_weights(width))
    lat = band(rows, EDGE).T
    eye = np.eye(BATCH)
    border = jnp.asarray(
        np.stack([np.kron(eye, lat[rows - EDGE :, rows + EDGE :]), np.kron(eye, lat[:EDGE, :EDGE])]).astype(BF)
    )
    lat = jnp.asarray(lat.copy())

    def shape(n, r=rows, c=width):
        return pltpu.VMEM((n, r, c), BF)

    def tiles(n, r=rows):
        return shape(n, r, LANES)

    dma = pltpu.SemaphoreType.DMA
    edge, inner, second, near, far, prod = call(
        first_kernel,
        "pack_edges",
        (ens, hbm(gradient)),
        [tiles(n_tiles, 2 * EDGE), tiles(n_tiles, rows - 2 * EDGE), tiles(n_tiles)]
        + [tiles(n_tiles, EDGE)] * 2
        + [shape(total)],
        scratch=[shape(levels), shape(8, width, 2 * LANES), shape(total), dma((1 + len(CHUNKS),))],
        specs=[ANYWHERE] * 2,
    )
    edge = first_partner(edge, "lon")
    inner = first_partner(inner, "lon")
    tnear, tfar = lat_exchange(near, far)
    near, far = call(rows_kernel, "edge_rows", (prod,), [shape(total, EDGE)] * 2)
    near, far = lat_exchange(near, far)
    sums = pltpu.VMEM((total, rows, width), jnp.float32)
    (acc,) = call(own_kernel, "own_sums", (prod, center, lat, tnear), [sums])
    (second,) = call(edge_lat_kernel, "edge_lat_sums", (second, tnear, tfar, lat, acc), [tiles(n_tiles)])
    second = second_partner(second, "lon", True)

    tnear, tfar = call(rows_kernel, "tile_rows", (edge, acc), [tiles(n_tiles, EDGE)] * 2, weight=HEAVY)
    tnear, tfar = lat_exchange(tnear, tfar)
    for is_near, rows_in in ((True, near), (False, far)):
        (acc,) = call(
            functools.partial(partner_kernel, is_near),
            "near_rows" if is_near else "far_rows",
            (acc, rows_in, center, border),
            [sums],
            aliases={0: 0},
        )
    (first,) = call(split_lat_kernel, "first_lat_sums", (edge, inner, tnear, tfar, lat, acc), [tiles(n_tiles)])
    (result,) = call(
        functools.partial(last_kernel, plan),
        "edge_sums",
        (acc, first, second, spread),
        [jax.ShapeDtypeStruct((total, rows, width), BF)],
        scratch=[shape(total), dma((len(plan),))],
        out_specs=[ANYWHERE],
    )
    return result.reshape(members, levels, rows, width)


def solution(mesh):
    placed = (P(None, None, "lat", "lon"), P(None, "lat", "lon"))
    return jax.shard_map(
        shards, mesh=mesh, in_specs=placed, out_specs=P(None, None, "lat", "lon"), check_vma=False
    )
```

```python
import functools

import jax
import jax.numpy as jnp
import numpy as np
from jax import lax
from jax.experimental import pallas as pl
from jax.experimental.pallas import tpu as pltpu
from jax.sharding import PartitionSpec as P

HALF = 30
LANES = 128
EDGE = 32
GROUP = 17
VMEM_LIMIT = 16 * 1024 * 1024
CHUNKS = (46, 34)
BATCH = 8
HEAVY = 25_000_000_000
BF = jnp.bfloat16


def taps():
    offsets = np.arange(-HALF, HALF + 1).astype(np.float32)
    spread = np.float32(HALF)
    norm = np.sqrt(np.sum(np.exp(-offsets * offsets / (spread * spread)), dtype=np.float32))
    return (np.exp(-offsets * offsets / (2 * spread * spread)) / norm).astype(BF)


def band(block_len, margin):
    k = taps()
    out = np.zeros((block_len + 2 * margin, block_len), BF)
    for q in range(block_len):
        out[q + margin - HALF : q + margin + HALF + 1, q] = k
    return out


def lon_weights(width):
    lon = band(width, HALF)
    spread = np.zeros((8, 2 * LANES, width), BF)
    for s in range(8):
        for j in range(HALF):
            lane = HALF * s + j if s < 4 else 120 + j - 8 * (s - 4)
            if s >= 4 and not 120 <= lane < 128:
                continue
            spread[s, lane] = lon[j]
            spread[s, LANES + lane] = lon[width + HALF + j]
    return lon[HALF : HALF + width].copy(), spread


def odd(axis):
    return lax.rem(lax.axis_index(axis), 2)


def fill_select(select_ref):
    width = select_ref.shape[1]
    side = odd("lon")
    row = lax.broadcasted_iota(jnp.int32, (width, 2 * LANES), 0)
    col = lax.broadcasted_iota(jnp.int32, (width, 2 * LANES), 1)
    diff = row - col
    end_tile, start_tile = side * LANES, (1 - side) * LANES
    for s in range(8):
        shift, lo, hi = (-HALF * s, HALF * s, HALF * s + HALF) if s < 4 else (8 * (s - 4) - 120, 120, 128)
        end = (diff == width - HALF + shift - end_tile) & (col >= end_tile + lo) & (col < end_tile + hi)
        start = (diff == shift - start_tile) & (col >= start_tile + lo) & (col < start_tile + hi) & (row < HALF)
        select_ref[s] = jnp.where(end | start, 1.0, 0.0).astype(BF)


def dot(a, b):
    return jnp.dot(a, b, preferred_element_type=jnp.float32)


def units(count):
    out, first = [], 0
    while count - first >= GROUP:
        out.append((first, 4, True))
        first += GROUP
    if count > first:
        out.append((first, (count - first) // 4, False))
    return out


def tiles_of(count):
    return sum(t for _, t, _ in units(count))


def stack(ref, first, count):
    return ref[first : first + count].reshape(count * ref.shape[1], ref.shape[2])


def pack(src_ref, unit, select_ref):
    first, n, extra = unit
    rows = src_ref.shape[1]
    acc = None
    for s in range(4):
        part = dot(stack(src_ref, first + s * n, n), select_ref[s])
        acc = part if acc is None else acc + part
    if extra:
        field = src_ref[first + 4 * n]
        acc += jnp.concatenate([dot(field, select_ref[4 + t]) for t in range(n)], axis=0)
    return acc.astype(BF).reshape(n, rows, 2 * LANES)


def product_and_pack(pieces, first, count, raw_ref, gvm_ref, select_ref, prod_ref, a_ref, b_ref):
    for f in range(first, first + count):
        level = f % gvm_ref.shape[0]
        grad = jnp.concatenate([gvm_ref[level, row : row + n] for row, n in pieces], axis=0)
        prod_ref[f] = (raw_ref[f].astype(jnp.float32) * grad.astype(jnp.float32)).astype(BF)
    for start, n, extra, tile in all_units(CHUNKS):
        if first <= start < first + count:
            tiles = pack(prod_ref, (start, n, extra), select_ref)
            a_ref[pl.ds(tile, n)] = tiles[:, :, :LANES]
            b_ref[pl.ds(tile, n)] = tiles[:, :, LANES:]


def edge_kernel(ens_ref, grad_ref, a_ref, b_ref, prod_ref, select_ref, gvm_ref, raw_ref, buf, sems):
    rows = ens_ref.shape[1]
    pieces = ((0, EDGE), (rows - EDGE, EDGE))
    grad = pltpu.make_async_copy(grad_ref, gvm_ref, sems.at[0])
    inner = pltpu.make_async_copy(ens_ref.at[:, pl.ds(EDGE, rows - 2 * EDGE)], raw_ref, sems.at[1])
    grad.start()
    copies = []
    start = 0
    for count in CHUNKS:
        at = pl.ds(start, count)
        for i, (row, n) in enumerate(pieces):
            from_ref, to_ref = ens_ref.at[at, pl.ds(row, n)], buf.at[at, pl.ds(i * EDGE, n)]
            copies.append(pltpu.make_async_copy(from_ref, to_ref, sems.at[2 + len(copies)]))
            copies[-1].start()
        start += count
    fill_select(select_ref)
    inner.start()
    grad.wait()
    start = 0
    for i, count in enumerate(CHUNKS):
        for copy in copies[2 * i : 2 * i + 2]:
            copy.wait()
        product_and_pack(pieces, start, count, buf, gvm_ref, select_ref, prod_ref, a_ref, b_ref)
        start += count
    inner.wait()


def inner_kernel(raw_ref, gvm_ref, select_ref, a_ref, b_ref, prod_ref):
    pieces = ((EDGE, raw_ref.shape[1]),)
    product_and_pack(pieces, 0, raw_ref.shape[0], raw_ref, gvm_ref, select_ref, prod_ref, a_ref, b_ref)


def emit_rows(v, near_ref, far_ref, at):
    up = odd("lat") == 0
    head, tail = v[:, :EDGE], v[:, v.shape[1] - EDGE :]
    near_ref[at] = jnp.where(up, tail, head)
    far_ref[at] = jnp.where(up, head, tail)


def rows_kernel(ref, *refs):
    near_ref, far_ref = refs[-2:]
    for f in range(0, ref.shape[0], 4):
        n = min(4, ref.shape[0] - f)
        emit_rows(ref[f : f + n], near_ref, far_ref, pl.ds(f, n))


def lat_field(field, low, high, lat_ref):
    return dot(lat_ref[...], jnp.concatenate([low, field, high], axis=0))


def lat_tiles(count, tile, near_ref, far_ref, lat_ref, out_ref):
    up = odd("lat") == 0
    for t in range(0, count, 2):
        n = min(2, count - t)
        field = jnp.concatenate([tile(i) for i in range(t, t + n)], axis=1)
        near, far = (jnp.concatenate([r[i] for i in range(t, t + n)], axis=1) for r in (near_ref, far_ref))
        done = lat_field(field, jnp.where(up, far, near), jnp.where(up, near, far), lat_ref).astype(BF)
        for i in range(n):
            out_ref[t + i] = done[:, i * LANES : (i + 1) * LANES]


def edge_lat_kernel(edge_ref, inner_ref, near_ref, far_ref, lat_ref, after_ref, out_ref):
    del after_ref

    def tile(t):
        return jnp.concatenate([edge_ref[t, :EDGE], inner_ref[t], edge_ref[t, EDGE:]], axis=0)

    lat_tiles(edge_ref.shape[0], tile, near_ref, far_ref, lat_ref, out_ref)


def add_rows(acc_ref, start, total, rows_ref, near, center_ref, border_ref):
    low = odd("lat") if near else 1 - odd("lat")
    edge = acc_ref.shape[1] - EDGE
    at = pl.ds(pl.multiple_of((1 - low) * edge, EDGE), EDGE)
    for first in range(start, start + total, BATCH):
        count = min(BATCH, start + total - first)
        own = dot(stack(rows_ref, first, count), center_ref[...]).astype(BF)
        part = dot(border_ref[low, : count * EDGE, : count * EDGE], own)
        for i in range(count):
            acc_ref[first + i, at] += part[i * EDGE : (i + 1) * EDGE]


def own_kernel(edge_ref, inner_ref, center_ref, lat_ref, after_ref, acc_ref):
    del after_ref
    rows = acc_ref.shape[1]
    for f in range(0, acc_ref.shape[0], 4):
        n = min(4, acc_ref.shape[0] - f)
        edge, inner = (
            dot(stack(ref, f, n), center_ref[...]).astype(BF).reshape(n, *ref.shape[1:]) for ref in (edge_ref, inner_ref)
        )
        for i in range(n):
            own = jnp.concatenate([edge[i, :EDGE], inner[i], edge[i, EDGE:]], axis=0)
            acc_ref[f + i] = dot(lat_ref[:, EDGE : EDGE + rows], own)


def partner_kernel(near, own_ref, rows_ref, center_ref, border_ref, acc_ref):
    del own_ref
    add_rows(acc_ref, 0, acc_ref.shape[0], rows_ref, near, center_ref, border_ref)


def last_kernel(plan, acc_ref, done_ref, tiles_ref, spread_ref, out_ref, buf, sem):
    rows, width = acc_ref.shape[1:]
    up = odd("lon") == 0

    def emit(first, n, v):
        at = pl.ds(first, n)
        buf[at] = (acc_ref[at].astype(jnp.float32) + v.reshape(n, rows, width)).astype(BF)
        pltpu.make_async_copy(buf.at[at], out_ref.at[at], sem).start()

    for first, n, extra, tile in plan:
        a, b = stack(done_ref, tile, n), stack(tiles_ref, tile, n)
        edges = jnp.concatenate([jnp.where(up, b, a), jnp.where(up, a, b)], axis=1)
        for s in range(4):
            emit(first + s * n, n, dot(edges, spread_ref[s]))
        if extra:
            parts = [dot(edges[t * rows : (t + 1) * rows], spread_ref[4 + t]) for t in range(n)]
            emit(first + 4 * n, 1, sum(parts[1:], parts[0]))
    pltpu.make_async_copy(buf, out_ref, sem).wait()


def all_units(counts):
    out, start, tile = [], 0, 0
    for count in counts:
        for first, n, extra in units(count):
            out.append((start + first, n, extra, tile))
            tile += n
        start += count
    return out


def first_partner(x, axis):
    return lax.ppermute(x, axis, [(i, i ^ 1) for i in range(lax.axis_size(axis))])


def second_partner(x, axis, periodic):
    count = lax.axis_size(axis)
    pairs = []
    for i in range(count):
        j = i + 1 if i % 2 else i - 1
        if periodic or 0 <= j < count:
            pairs.append((i, j % count))
    return lax.ppermute(x, axis, pairs)


def lat_exchange(near, far):
    return first_partner(near, "lat"), second_partner(far, "lat", False)


IN_VMEM = pl.BlockSpec(memory_space=pltpu.VMEM)
ANYWHERE = pl.BlockSpec(memory_space=pl.ANY)


def vm(x):
    return pltpu.with_memory_space_constraint(x, pltpu.VMEM)


def hbm(x):
    return pltpu.with_memory_space_constraint(x, pltpu.HBM)


def call(kernel, name, args, outs, scratch=(), specs=None, out_specs=None, aliases=None, weight=0):
    return pl.pallas_call(
        kernel,
        in_specs=specs or [IN_VMEM] * len(args),
        out_specs=out_specs or [IN_VMEM] * len(outs),
        out_shape=outs,
        scratch_shapes=list(scratch),
        input_output_aliases=aliases or {},
        compiler_params=pltpu.CompilerParams(vmem_limit_bytes=VMEM_LIMIT),
        cost_estimate=pl.CostEstimate(flops=weight, bytes_accessed=weight, transcendentals=0),
        name=name,
    )(*[vm(a) if specs is None or specs[i] is IN_VMEM else a for i, a in enumerate(args)])


def shards(ensemble, gradient):
    members, levels, rows, width = ensemble.shape
    total = members * levels
    ens = hbm(ensemble.reshape(total, rows, width))
    plan = all_units(CHUNKS)
    n_tiles = sum(n for _, n, _, _ in plan)
    center, spread = map(jnp.asarray, lon_weights(width))
    lat = band(rows, EDGE).T
    eye = np.eye(BATCH)
    border = jnp.asarray(
        np.stack([np.kron(eye, lat[rows - EDGE :, rows + EDGE :]), np.kron(eye, lat[:EDGE, :EDGE])]).astype(BF)
    )
    lat = jnp.asarray(lat.copy())

    def shape(n, r=rows, c=width):
        return pltpu.VMEM((n, r, c), BF)

    def tiles(n, r=rows):
        return shape(n, r, LANES)

    dma = pltpu.SemaphoreType.DMA
    between = rows - 2 * EDGE
    edge, b_edge, prod_edge, select, grad, raw = call(
        edge_kernel,
        "pack_edge_rows",
        (ens, hbm(gradient)),
        [
            tiles(n_tiles, 2 * EDGE),
            tiles(n_tiles, 2 * EDGE),
            shape(total, 2 * EDGE),
            shape(8, width, 2 * LANES),
            shape(levels),
            shape(total, between),
        ],
        scratch=[shape(total, 2 * EDGE), dma((2 + 2 * len(CHUNKS),))],
        specs=[ANYWHERE] * 2,
    )
    edge = first_partner(edge, "lon")
    near, far = call(rows_kernel, "packed_rows", (b_edge,), [tiles(n_tiles, EDGE)] * 2)
    tnear, tfar = lat_exchange(near, far)
    inner, b_inner, prod_inner = call(
        inner_kernel,
        "pack_inner_rows",
        (raw, grad, select),
        [tiles(n_tiles, between), tiles(n_tiles, between), shape(total, between)],
    )
    inner = first_partner(inner, "lon")
    near, far = call(rows_kernel, "edge_rows", (prod_edge, b_inner), [shape(total, EDGE)] * 2)
    near, far = lat_exchange(near, far)
    sums = pltpu.VMEM((total, rows, width), jnp.float32)
    (payload,) = call(edge_lat_kernel, "edge_lat_sums", (b_edge, b_inner, tnear, tfar, lat, tnear), [tiles(n_tiles)])
    (acc,) = call(own_kernel, "own_sums", (prod_edge, prod_inner, center, lat, edge), [sums])
    second = second_partner(payload, "lon", True)

    tnear, tfar = call(rows_kernel, "tile_rows", (edge, acc), [tiles(n_tiles, EDGE)] * 2, weight=HEAVY)
    tnear, tfar = lat_exchange(tnear, tfar)
    for is_near, rows_in in ((True, near), (False, far)):
        (acc,) = call(
            functools.partial(partner_kernel, is_near),
            "near_rows" if is_near else "far_rows",
            (acc, rows_in, center, border),
            [sums],
            aliases={0: 0},
        )
    (first,) = call(edge_lat_kernel, "first_lat_sums", (edge, inner, tnear, tfar, lat, acc), [tiles(n_tiles)])
    (result,) = call(
        functools.partial(last_kernel, plan),
        "edge_sums",
        (acc, first, second, spread),
        [jax.ShapeDtypeStruct((total, rows, width), BF)],
        scratch=[shape(total), dma],
        out_specs=[ANYWHERE],
    )
    return result.reshape(members, levels, rows, width)


def solution(mesh):
    placed = (P(None, None, "lat", "lon"), P(None, "lat", "lon"))
    return jax.shard_map(
        shards, mesh=mesh, in_specs=placed, out_specs=P(None, None, "lat", "lon"), check_vma=False
    )
```

```python
import functools

import jax
import jax.numpy as jnp
import numpy as np
from jax import lax
from jax.experimental import pallas as pl
from jax.experimental.pallas import tpu as pltpu
from jax.sharding import PartitionSpec as P

HALF = 30
LANES = 128
EDGE = 32
GROUP = 17
VMEM_LIMIT = 16 * 1024 * 1024
CHUNKS = (46, 34)
BATCH = 8
HEAVY = 25_000_000_000
BF = jnp.bfloat16


def taps():
    offsets = np.arange(-HALF, HALF + 1).astype(np.float32)
    spread = np.float32(HALF)
    norm = np.sqrt(np.sum(np.exp(-offsets * offsets / (spread * spread)), dtype=np.float32))
    return (np.exp(-offsets * offsets / (2 * spread * spread)) / norm).astype(BF)


def band(block_len, margin):
    k = taps()
    out = np.zeros((block_len + 2 * margin, block_len), BF)
    for q in range(block_len):
        out[q + margin - HALF : q + margin + HALF + 1, q] = k
    return out


def lon_weights(width):
    lon = band(width, HALF)
    spread = np.zeros((8, 2 * LANES, width), BF)
    for s in range(8):
        for j in range(HALF):
            lane = HALF * s + j if s < 4 else 120 + j - 8 * (s - 4)
            if s >= 4 and not 120 <= lane < 128:
                continue
            spread[s, lane] = lon[j]
            spread[s, LANES + lane] = lon[width + HALF + j]
    return lon[HALF : HALF + width].copy(), spread


def odd(axis):
    return lax.rem(lax.axis_index(axis), 2)


def fill_select(select_ref):
    width = select_ref.shape[1]
    side = odd("lon")
    row = lax.broadcasted_iota(jnp.int32, (width, 2 * LANES), 0)
    col = lax.broadcasted_iota(jnp.int32, (width, 2 * LANES), 1)
    diff = row - col
    end_tile, start_tile = side * LANES, (1 - side) * LANES
    for s in range(8):
        shift, lo, hi = (-HALF * s, HALF * s, HALF * s + HALF) if s < 4 else (8 * (s - 4) - 120, 120, 128)
        end = (diff == width - HALF + shift - end_tile) & (col >= end_tile + lo) & (col < end_tile + hi)
        start = (diff == shift - start_tile) & (col >= start_tile + lo) & (col < start_tile + hi) & (row < HALF)
        select_ref[s] = jnp.where(end | start, 1.0, 0.0).astype(BF)


def dot(a, b):
    return jnp.dot(a, b, preferred_element_type=jnp.float32)


def units(count):
    out, first = [], 0
    while count - first >= GROUP:
        out.append((first, 4, True))
        first += GROUP
    if count > first:
        out.append((first, (count - first) // 4, False))
    return out


def tiles_of(count):
    return sum(t for _, t, _ in units(count))


def stack(ref, first, count):
    return ref[first : first + count].reshape(count * ref.shape[1], ref.shape[2])


def pack(src_ref, unit, select_ref):
    first, n, extra = unit
    rows = src_ref.shape[1]
    acc = None
    for s in range(4):
        part = dot(stack(src_ref, first + s * n, n), select_ref[s])
        acc = part if acc is None else acc + part
    if extra:
        field = src_ref[first + 4 * n]
        acc += jnp.concatenate([dot(field, select_ref[4 + t]) for t in range(n)], axis=0)
    return acc.astype(BF).reshape(n, rows, 2 * LANES)


def product_and_pack(pieces, first, count, raw_ref, gvm_ref, select_ref, prod_ref, a_ref, b_ref):
    for f in range(first, first + count):
        level = f % gvm_ref.shape[0]
        grad = jnp.concatenate([gvm_ref[level, row : row + n] for row, n in pieces], axis=0)
        prod_ref[f] = (raw_ref[f].astype(jnp.float32) * grad.astype(jnp.float32)).astype(BF)
    for start, n, extra, tile in all_units(CHUNKS):
        if first <= start < first + count:
            tiles = pack(prod_ref, (start, n, extra), select_ref)
            a_ref[pl.ds(tile, n)] = tiles[:, :, :LANES]
            b_ref[pl.ds(tile, n)] = tiles[:, :, LANES:]


def edge_kernel(ens_ref, grad_ref, a_ref, b_ref, prod_ref, select_ref, gvm_ref, raw_ref, buf, sems):
    rows = ens_ref.shape[1]
    pieces = ((0, EDGE), (rows - EDGE, EDGE))
    grad = pltpu.make_async_copy(grad_ref, gvm_ref, sems.at[0])
    inner = pltpu.make_async_copy(ens_ref.at[:, pl.ds(EDGE, rows - 2 * EDGE)], raw_ref, sems.at[1])
    grad.start()
    copies = []
    start = 0
    for count in CHUNKS:
        at = pl.ds(start, count)
        for i, (row, n) in enumerate(pieces):
            from_ref, to_ref = ens_ref.at[at, pl.ds(row, n)], buf.at[at, pl.ds(i * EDGE, n)]
            copies.append(pltpu.make_async_copy(from_ref, to_ref, sems.at[2 + len(copies)]))
            copies[-1].start()
        start += count
    fill_select(select_ref)
    inner.start()
    grad.wait()
    start = 0
    for i, count in enumerate(CHUNKS):
        for copy in copies[2 * i : 2 * i + 2]:
            copy.wait()
        product_and_pack(pieces, start, count, buf, gvm_ref, select_ref, prod_ref, a_ref, b_ref)
        start += count
    inner.wait()


def inner_kernel(raw_ref, gvm_ref, select_ref, a_ref, b_ref, prod_ref):
    pieces = ((EDGE, raw_ref.shape[1]),)
    product_and_pack(pieces, 0, raw_ref.shape[0], raw_ref, gvm_ref, select_ref, prod_ref, a_ref, b_ref)


def emit_rows(v, near_ref, far_ref, at):
    up = odd("lat") == 0
    head, tail = v[:, :EDGE], v[:, v.shape[1] - EDGE :]
    near_ref[at] = jnp.where(up, tail, head)
    far_ref[at] = jnp.where(up, head, tail)


def rows_kernel(ref, *refs):
    near_ref, far_ref = refs[-2:]
    for f in range(0, ref.shape[0], 4):
        n = min(4, ref.shape[0] - f)
        emit_rows(ref[f : f + n], near_ref, far_ref, pl.ds(f, n))


def lat_field(field, low, high, lat_ref):
    return dot(lat_ref[...], jnp.concatenate([low, field, high], axis=0))


def lat_tiles(count, tile, near_ref, far_ref, lat_ref, out_ref):
    up = odd("lat") == 0
    for t in range(0, count, 2):
        n = min(2, count - t)
        field = jnp.concatenate([tile(i) for i in range(t, t + n)], axis=1)
        near, far = (jnp.concatenate([r[i] for i in range(t, t + n)], axis=1) for r in (near_ref, far_ref))
        done = lat_field(field, jnp.where(up, far, near), jnp.where(up, near, far), lat_ref).astype(BF)
        for i in range(n):
            out_ref[t + i] = done[:, i * LANES : (i + 1) * LANES]


def edge_lat_kernel(edge_ref, inner_ref, near_ref, far_ref, lat_ref, after_ref, out_ref):
    del after_ref

    def tile(t):
        return jnp.concatenate([edge_ref[t, :EDGE], inner_ref[t], edge_ref[t, EDGE:]], axis=0)

    lat_tiles(edge_ref.shape[0], tile, near_ref, far_ref, lat_ref, out_ref)


def add_rows(acc_ref, start, total, rows_ref, near, center_ref, border_ref):
    low = odd("lat") if near else 1 - odd("lat")
    edge = acc_ref.shape[1] - EDGE
    at = pl.ds(pl.multiple_of((1 - low) * edge, EDGE), EDGE)
    for first in range(start, start + total, BATCH):
        count = min(BATCH, start + total - first)
        own = dot(stack(rows_ref, first, count), center_ref[...]).astype(BF)
        part = dot(border_ref[low, : count * EDGE, : count * EDGE], own)
        for i in range(count):
            acc_ref[first + i, at] += part[i * EDGE : (i + 1) * EDGE]


def own_kernel(edge_ref, inner_ref, center_ref, lat_ref, after_ref, acc_ref):
    del after_ref
    rows = acc_ref.shape[1]
    for f in range(0, acc_ref.shape[0], 4):
        n = min(4, acc_ref.shape[0] - f)
        edge, inner = (
            dot(stack(ref, f, n), center_ref[...]).astype(BF).reshape(n, *ref.shape[1:]) for ref in (edge_ref, inner_ref)
        )
        for i in range(n):
            own = jnp.concatenate([edge[i, :EDGE], inner[i], edge[i, EDGE:]], axis=0)
            acc_ref[f + i] = dot(lat_ref[:, EDGE : EDGE + rows], own)


def partner_kernel(near, own_ref, rows_ref, center_ref, border_ref, acc_ref):
    del own_ref
    add_rows(acc_ref, 0, acc_ref.shape[0], rows_ref, near, center_ref, border_ref)


def last_kernel(plan, acc_ref, done_ref, tiles_ref, spread_ref, out_ref, buf, sem):
    rows, width = acc_ref.shape[1:]
    up = odd("lon") == 0

    def emit(first, n, v):
        at = pl.ds(first, n)
        buf[at] = (acc_ref[at].astype(jnp.float32) + v.reshape(n, rows, width)).astype(BF)
        pltpu.make_async_copy(buf.at[at], out_ref.at[at], sem).start()

    for first, n, extra, tile in plan:
        a, b = stack(done_ref, tile, n), stack(tiles_ref, tile, n)
        edges = jnp.concatenate([jnp.where(up, b, a), jnp.where(up, a, b)], axis=1)
        for s in range(4):
            emit(first + s * n, n, dot(edges, spread_ref[s]))
        if extra:
            parts = [dot(edges[t * rows : (t + 1) * rows], spread_ref[4 + t]) for t in range(n)]
            emit(first + 4 * n, 1, sum(parts[1:], parts[0]))
    pltpu.make_async_copy(buf, out_ref, sem).wait()


def all_units(counts):
    out, start, tile = [], 0, 0
    for count in counts:
        for first, n, extra in units(count):
            out.append((start + first, n, extra, tile))
            tile += n
        start += count
    return out


def first_partner(x, axis):
    return lax.ppermute(x, axis, [(i, i ^ 1) for i in range(lax.axis_size(axis))])


def second_partner(x, axis, periodic):
    count = lax.axis_size(axis)
    pairs = []
    for i in range(count):
        j = i + 1 if i % 2 else i - 1
        if periodic or 0 <= j < count:
            pairs.append((i, j % count))
    return lax.ppermute(x, axis, pairs)


def lat_exchange(near, far):
    return first_partner(near, "lat"), second_partner(far, "lat", False)


IN_VMEM = pl.BlockSpec(memory_space=pltpu.VMEM)
ANYWHERE = pl.BlockSpec(memory_space=pl.ANY)


def vm(x):
    return pltpu.with_memory_space_constraint(x, pltpu.VMEM)


def hbm(x):
    return pltpu.with_memory_space_constraint(x, pltpu.HBM)


def call(kernel, name, args, outs, scratch=(), specs=None, out_specs=None, aliases=None, weight=0):
    return pl.pallas_call(
        kernel,
        in_specs=specs or [IN_VMEM] * len(args),
        out_specs=out_specs or [IN_VMEM] * len(outs),
        out_shape=outs,
        scratch_shapes=list(scratch),
        input_output_aliases=aliases or {},
        compiler_params=pltpu.CompilerParams(vmem_limit_bytes=VMEM_LIMIT),
        cost_estimate=pl.CostEstimate(flops=weight, bytes_accessed=weight, transcendentals=0),
        name=name,
    )(*[vm(a) if specs is None or specs[i] is IN_VMEM else a for i, a in enumerate(args)])


def shards(ensemble, gradient):
    members, levels, rows, width = ensemble.shape
    total = members * levels
    ens = hbm(ensemble.reshape(total, rows, width))
    plan = all_units(CHUNKS)
    n_tiles = sum(n for _, n, _, _ in plan)
    center, spread = map(jnp.asarray, lon_weights(width))
    lat = band(rows, EDGE).T
    eye = np.eye(BATCH)
    border = jnp.asarray(
        np.stack([np.kron(eye, lat[rows - EDGE :, rows + EDGE :]), np.kron(eye, lat[:EDGE, :EDGE])]).astype(BF)
    )
    lat = jnp.asarray(lat.copy())

    def shape(n, r=rows, c=width):
        return pltpu.VMEM((n, r, c), BF)

    def tiles(n, r=rows):
        return shape(n, r, LANES)

    dma = pltpu.SemaphoreType.DMA
    between = rows - 2 * EDGE
    edge, b_edge, prod_edge, select, grad, raw = call(
        edge_kernel,
        "pack_edge_rows",
        (ens, hbm(gradient)),
        [
            tiles(n_tiles, 2 * EDGE),
            tiles(n_tiles, 2 * EDGE),
            shape(total, 2 * EDGE),
            shape(8, width, 2 * LANES),
            shape(levels),
            shape(total, between),
        ],
        scratch=[shape(total, 2 * EDGE), dma((2 + 2 * len(CHUNKS),))],
        specs=[ANYWHERE] * 2,
    )
    edge = first_partner(edge, "lon")
    near, far = call(rows_kernel, "packed_rows", (b_edge,), [tiles(n_tiles, EDGE)] * 2)
    tnear, tfar = lat_exchange(near, far)
    inner, b_inner, prod_inner = call(
        inner_kernel,
        "pack_inner_rows",
        (raw, grad, select),
        [tiles(n_tiles, between), tiles(n_tiles, between), shape(total, between)],
    )
    inner = first_partner(inner, "lon")
    near, far = call(rows_kernel, "edge_rows", (prod_edge, b_inner), [shape(total, EDGE)] * 2)
    near, far = lat_exchange(near, far)
    sums = pltpu.VMEM((total, rows, width), jnp.float32)
    (payload,) = call(edge_lat_kernel, "edge_lat_sums", (b_edge, b_inner, tnear, tfar, lat, tnear), [tiles(n_tiles)])
    (acc,) = call(own_kernel, "own_sums", (prod_edge, prod_inner, center, lat, edge), [sums])
    second = second_partner(payload, "lon", True)

    tnear, tfar = call(rows_kernel, "tile_rows", (edge, acc), [tiles(n_tiles, EDGE)] * 2, weight=HEAVY)
    tnear, tfar = lat_exchange(tnear, tfar)
    for is_near, rows_in in ((True, near), (False, far)):
        (acc,) = call(
            functools.partial(partner_kernel, is_near),
            "near_rows" if is_near else "far_rows",
            (acc, rows_in, center, border),
            [sums],
            aliases={0: 0},
        )
    (first,) = call(edge_lat_kernel, "first_lat_sums", (edge, inner, tnear, tfar, lat, acc), [tiles(n_tiles)])
    (result,) = call(
        functools.partial(last_kernel, sorted(plan, key=lambda unit: unit[1])),
        "edge_sums",
        (acc, first, second, spread),
        [jax.ShapeDtypeStruct((total, rows, width), BF)],
        scratch=[shape(total), dma],
        out_specs=[ANYWHERE],
    )
    return result.reshape(members, levels, rows, width)


def solution(mesh):
    placed = (P(None, None, "lat", "lon"), P(None, "lat", "lon"))
    return jax.shard_map(
        shards, mesh=mesh, in_specs=placed, out_specs=P(None, None, "lat", "lon"), check_vma=False
    )
```

```python
import functools

import jax
import jax.numpy as jnp
import numpy as np
from jax import lax
from jax.experimental import pallas as pl
from jax.experimental.pallas import tpu as pltpu
from jax.sharding import PartitionSpec as P

HALF = 30
LANES = 128
EDGE = 32
GROUP = 17
VMEM_LIMIT = 16 * 1024 * 1024
CHUNKS = (46, 34)
BATCH = 8
HEAVY = 25_000_000_000
BF = jnp.bfloat16


def taps():
    offsets = np.arange(-HALF, HALF + 1).astype(np.float32)
    spread = np.float32(HALF)
    norm = np.sqrt(np.sum(np.exp(-offsets * offsets / (spread * spread)), dtype=np.float32))
    return (np.exp(-offsets * offsets / (2 * spread * spread)) / norm).astype(BF)


def band(block_len, margin):
    k = taps()
    out = np.zeros((block_len + 2 * margin, block_len), BF)
    for q in range(block_len):
        out[q + margin - HALF : q + margin + HALF + 1, q] = k
    return out


def lon_weights(width):
    lon = band(width, HALF)
    spread = np.zeros((8, 2 * LANES, width), BF)
    for s in range(8):
        for j in range(HALF):
            lane = HALF * s + j if s < 4 else 120 + j - 8 * (s - 4)
            if s >= 4 and not 120 <= lane < 128:
                continue
            spread[s, lane] = lon[j]
            spread[s, LANES + lane] = lon[width + HALF + j]
    return lon[HALF : HALF + width].copy(), spread


def odd(axis):
    return lax.rem(lax.axis_index(axis), 2)


def fill_select(select_ref):
    width = select_ref.shape[1]
    side = odd("lon")
    row = lax.broadcasted_iota(jnp.int32, (width, 2 * LANES), 0)
    col = lax.broadcasted_iota(jnp.int32, (width, 2 * LANES), 1)
    diff = row - col
    end_tile, start_tile = side * LANES, (1 - side) * LANES
    for s in range(8):
        shift, lo, hi = (-HALF * s, HALF * s, HALF * s + HALF) if s < 4 else (8 * (s - 4) - 120, 120, 128)
        end = (diff == width - HALF + shift - end_tile) & (col >= end_tile + lo) & (col < end_tile + hi)
        start = (diff == shift - start_tile) & (col >= start_tile + lo) & (col < start_tile + hi) & (row < HALF)
        select_ref[s] = jnp.where(end | start, 1.0, 0.0).astype(BF)


def dot(a, b):
    return jnp.dot(a, b, preferred_element_type=jnp.float32)


def units(count):
    out, first = [], 0
    while count - first >= GROUP:
        out.append((first, 4, True))
        first += GROUP
    if count > first:
        out.append((first, (count - first) // 4, False))
    return out


def tiles_of(count):
    return sum(t for _, t, _ in units(count))


def stack(ref, first, count):
    return ref[first : first + count].reshape(count * ref.shape[1], ref.shape[2])


def pack(src_ref, unit, select_ref):
    first, n, extra = unit
    rows = src_ref.shape[1]
    acc = None
    for s in range(4):
        part = dot(stack(src_ref, first + s * n, n), select_ref[s])
        acc = part if acc is None else acc + part
    if extra:
        field = src_ref[first + 4 * n]
        acc += jnp.concatenate([dot(field, select_ref[4 + t]) for t in range(n)], axis=0)
    return acc.astype(BF).reshape(n, rows, 2 * LANES)


def product_and_pack(pieces, first, count, raw_ref, gvm_ref, select_ref, prod_ref, a_ref, b_ref):
    for f in range(first, first + count):
        level = f % gvm_ref.shape[0]
        grad = jnp.concatenate([gvm_ref[level, row : row + n] for row, n in pieces], axis=0)
        prod_ref[f] = raw_ref[f] * grad
    for start, n, extra, tile in all_units(CHUNKS):
        if first <= start < first + count:
            tiles = pack(prod_ref, (start, n, extra), select_ref)
            a_ref[pl.ds(tile, n)] = tiles[:, :, :LANES]
            b_ref[pl.ds(tile, n)] = tiles[:, :, LANES:]


def edge_kernel(ens_ref, grad_ref, a_ref, b_ref, prod_ref, select_ref, gvm_ref, raw_ref, buf, sems):
    rows = ens_ref.shape[1]
    pieces = ((0, EDGE), (rows - EDGE, EDGE))
    grad = pltpu.make_async_copy(grad_ref, gvm_ref, sems.at[0])
    inner = pltpu.make_async_copy(ens_ref.at[:, pl.ds(EDGE, rows - 2 * EDGE)], raw_ref, sems.at[1])
    grad.start()
    copies = []
    start = 0
    for count in CHUNKS:
        at = pl.ds(start, count)
        for i, (row, n) in enumerate(pieces):
            from_ref, to_ref = ens_ref.at[at, pl.ds(row, n)], buf.at[at, pl.ds(i * EDGE, n)]
            copies.append(pltpu.make_async_copy(from_ref, to_ref, sems.at[2 + len(copies)]))
            copies[-1].start()
        start += count
    fill_select(select_ref)
    inner.start()
    grad.wait()
    start = 0
    for i, count in enumerate(CHUNKS):
        for copy in copies[2 * i : 2 * i + 2]:
            copy.wait()
        product_and_pack(pieces, start, count, buf, gvm_ref, select_ref, prod_ref, a_ref, b_ref)
        start += count
    inner.wait()


def inner_kernel(raw_ref, gvm_ref, select_ref, a_ref, b_ref, prod_ref):
    pieces = ((EDGE, raw_ref.shape[1]),)
    product_and_pack(pieces, 0, raw_ref.shape[0], raw_ref, gvm_ref, select_ref, prod_ref, a_ref, b_ref)


def emit_rows(v, near_ref, far_ref, at):
    up = odd("lat") == 0
    head, tail = v[:, :EDGE], v[:, v.shape[1] - EDGE :]
    near_ref[at] = jnp.where(up, tail, head)
    far_ref[at] = jnp.where(up, head, tail)


def rows_kernel(ref, *refs):
    near_ref, far_ref = refs[-2:]
    for f in range(0, ref.shape[0], 4):
        n = min(4, ref.shape[0] - f)
        emit_rows(ref[f : f + n], near_ref, far_ref, pl.ds(f, n))


def lat_field(field, low, high, lat_ref):
    return dot(lat_ref[...], jnp.concatenate([low, field, high], axis=0))


def lat_tiles(count, tile, near_ref, far_ref, lat_ref, out_ref):
    up = odd("lat") == 0
    for t in range(0, count, 2):
        n = min(2, count - t)
        field = jnp.concatenate([tile(i) for i in range(t, t + n)], axis=1)
        near, far = (jnp.concatenate([r[i] for i in range(t, t + n)], axis=1) for r in (near_ref, far_ref))
        done = lat_field(field, jnp.where(up, far, near), jnp.where(up, near, far), lat_ref).astype(BF)
        for i in range(n):
            out_ref[t + i] = done[:, i * LANES : (i + 1) * LANES]


def edge_lat_kernel(edge_ref, inner_ref, near_ref, far_ref, lat_ref, after_ref, out_ref):
    del after_ref

    def tile(t):
        return jnp.concatenate([edge_ref[t, :EDGE], inner_ref[t], edge_ref[t, EDGE:]], axis=0)

    lat_tiles(edge_ref.shape[0], tile, near_ref, far_ref, lat_ref, out_ref)


def add_rows(acc_ref, start, total, rows_ref, near, center_ref, border_ref):
    low = odd("lat") if near else 1 - odd("lat")
    edge = acc_ref.shape[1] - EDGE
    at = pl.ds(pl.multiple_of((1 - low) * edge, EDGE), EDGE)
    for first in range(start, start + total, BATCH):
        count = min(BATCH, start + total - first)
        own = dot(stack(rows_ref, first, count), center_ref[...]).astype(BF)
        part = dot(border_ref[low, : count * EDGE, : count * EDGE], own)
        for i in range(count):
            acc_ref[first + i, at] += part[i * EDGE : (i + 1) * EDGE]


def own_kernel(edge_ref, inner_ref, center_ref, lat_ref, after_ref, acc_ref):
    del after_ref
    rows = acc_ref.shape[1]
    for f in range(0, acc_ref.shape[0], 4):
        n = min(4, acc_ref.shape[0] - f)
        edge, inner = (
            dot(stack(ref, f, n), center_ref[...]).astype(BF).reshape(n, *ref.shape[1:]) for ref in (edge_ref, inner_ref)
        )
        for i in range(n):
            own = jnp.concatenate([edge[i, :EDGE], inner[i], edge[i, EDGE:]], axis=0)
            acc_ref[f + i] = dot(lat_ref[:, EDGE : EDGE + rows], own)


def partner_kernel(near, own_ref, rows_ref, center_ref, border_ref, acc_ref):
    del own_ref
    add_rows(acc_ref, 0, acc_ref.shape[0], rows_ref, near, center_ref, border_ref)


def last_kernel(plan, acc_ref, done_ref, tiles_ref, spread_ref, out_ref, buf, sem):
    rows, width = acc_ref.shape[1:]
    up = odd("lon") == 0

    def emit(first, n, v):
        at = pl.ds(first, n)
        buf[at] = (acc_ref[at].astype(jnp.float32) + v.reshape(n, rows, width)).astype(BF)
        pltpu.make_async_copy(buf.at[at], out_ref.at[at], sem).start()

    for first, n, extra, tile in plan:
        a, b = stack(done_ref, tile, n), stack(tiles_ref, tile, n)
        edges = jnp.concatenate([jnp.where(up, b, a), jnp.where(up, a, b)], axis=1)
        for s in range(4):
            emit(first + s * n, n, dot(edges, spread_ref[s]))
        if extra:
            parts = [dot(edges[t * rows : (t + 1) * rows], spread_ref[4 + t]) for t in range(n)]
            emit(first + 4 * n, 1, sum(parts[1:], parts[0]))
    pltpu.make_async_copy(buf, out_ref, sem).wait()


def all_units(counts):
    out, start, tile = [], 0, 0
    for count in counts:
        for first, n, extra in units(count):
            out.append((start + first, n, extra, tile))
            tile += n
        start += count
    return out


def first_partner(x, axis):
    return lax.ppermute(x, axis, [(i, i ^ 1) for i in range(lax.axis_size(axis))])


def second_partner(x, axis, periodic):
    count = lax.axis_size(axis)
    pairs = []
    for i in range(count):
        j = i + 1 if i % 2 else i - 1
        if periodic or 0 <= j < count:
            pairs.append((i, j % count))
    return lax.ppermute(x, axis, pairs)


def lat_exchange(near, far):
    return first_partner(near, "lat"), second_partner(far, "lat", False)


IN_VMEM = pl.BlockSpec(memory_space=pltpu.VMEM)
ANYWHERE = pl.BlockSpec(memory_space=pl.ANY)


def vm(x):
    return pltpu.with_memory_space_constraint(x, pltpu.VMEM)


def hbm(x):
    return pltpu.with_memory_space_constraint(x, pltpu.HBM)


def call(kernel, name, args, outs, scratch=(), specs=None, out_specs=None, aliases=None, weight=0):
    return pl.pallas_call(
        kernel,
        in_specs=specs or [IN_VMEM] * len(args),
        out_specs=out_specs or [IN_VMEM] * len(outs),
        out_shape=outs,
        scratch_shapes=list(scratch),
        input_output_aliases=aliases or {},
        compiler_params=pltpu.CompilerParams(vmem_limit_bytes=VMEM_LIMIT),
        cost_estimate=pl.CostEstimate(flops=weight, bytes_accessed=weight, transcendentals=0),
        name=name,
    )(*[vm(a) if specs is None or specs[i] is IN_VMEM else a for i, a in enumerate(args)])


def shards(ensemble, gradient):
    members, levels, rows, width = ensemble.shape
    total = members * levels
    ens = hbm(ensemble.reshape(total, rows, width))
    plan = all_units(CHUNKS)
    n_tiles = sum(n for _, n, _, _ in plan)
    center, spread = map(jnp.asarray, lon_weights(width))
    lat = band(rows, EDGE).T
    eye = np.eye(BATCH)
    border = jnp.asarray(
        np.stack([np.kron(eye, lat[rows - EDGE :, rows + EDGE :]), np.kron(eye, lat[:EDGE, :EDGE])]).astype(BF)
    )
    lat = jnp.asarray(lat.copy())

    def shape(n, r=rows, c=width):
        return pltpu.VMEM((n, r, c), BF)

    def tiles(n, r=rows):
        return shape(n, r, LANES)

    dma = pltpu.SemaphoreType.DMA
    between = rows - 2 * EDGE
    edge, b_edge, prod_edge, select, grad, raw = call(
        edge_kernel,
        "pack_edge_rows",
        (ens, hbm(gradient)),
        [
            tiles(n_tiles, 2 * EDGE),
            tiles(n_tiles, 2 * EDGE),
            shape(total, 2 * EDGE),
            shape(8, width, 2 * LANES),
            shape(levels),
            shape(total, between),
        ],
        scratch=[shape(total, 2 * EDGE), dma((2 + 2 * len(CHUNKS),))],
        specs=[ANYWHERE] * 2,
    )
    edge = first_partner(edge, "lon")
    near, far = call(rows_kernel, "packed_rows", (b_edge,), [tiles(n_tiles, EDGE)] * 2)
    tnear, tfar = lat_exchange(near, far)
    inner, b_inner, prod_inner = call(
        inner_kernel,
        "pack_inner_rows",
        (raw, grad, select),
        [tiles(n_tiles, between), tiles(n_tiles, between), shape(total, between)],
    )
    inner = first_partner(inner, "lon")
    near, far = call(rows_kernel, "edge_rows", (prod_edge, b_inner), [shape(total, EDGE)] * 2)
    near, far = lat_exchange(near, far)
    sums = pltpu.VMEM((total, rows, width), jnp.float32)
    (payload,) = call(edge_lat_kernel, "edge_lat_sums", (b_edge, b_inner, tnear, tfar, lat, tnear), [tiles(n_tiles)])
    (acc,) = call(own_kernel, "own_sums", (prod_edge, prod_inner, center, lat, edge), [sums])
    second = second_partner(payload, "lon", True)

    tnear, tfar = call(rows_kernel, "tile_rows", (edge, acc), [tiles(n_tiles, EDGE)] * 2, weight=HEAVY)
    tnear, tfar = lat_exchange(tnear, tfar)
    for is_near, rows_in in ((True, near), (False, far)):
        (acc,) = call(
            functools.partial(partner_kernel, is_near),
            "near_rows" if is_near else "far_rows",
            (acc, rows_in, center, border),
            [sums],
            aliases={0: 0},
        )
    (first,) = call(edge_lat_kernel, "first_lat_sums", (edge, inner, tnear, tfar, lat, acc), [tiles(n_tiles)])
    (result,) = call(
        functools.partial(last_kernel, sorted(plan, key=lambda unit: unit[1])),
        "edge_sums",
        (acc, first, second, spread),
        [jax.ShapeDtypeStruct((total, rows, width), BF)],
        scratch=[shape(total), dma],
        out_specs=[ANYWHERE],
    )
    return result.reshape(members, levels, rows, width)


def solution(mesh):
    placed = (P(None, None, "lat", "lon"), P(None, "lat", "lon"))
    return jax.shard_map(
        shards, mesh=mesh, in_specs=placed, out_specs=P(None, None, "lat", "lon"), check_vma=False
    )
```
